128 devices in a mesh: section: 8 (over y_lo, z), head: 16 (over x, y_hi, core).
Axes of the slice: x: 4, y: 4 (y_hi: 2, y_lo: 2; y = y_hi * 2 + y_lo), z: 4, core: 2. Of those that a mesh axis runs over, the one named last changes fastest.
Arguments:
- section_inputs: bfloat16 [8, 256, 1024], P('section'), may hold values from -6 to 6
- section_cotangents: bfloat16 [8, 256, 1024], P('section'), may hold values from -6 to 6
- fresh_tokens: bfloat16 [2, 256, 1024], replicated, may hold values from -6 to 6
- fresh_cotangents: bfloat16 [2, 256, 1024], replicated, may hold values from -6 to 6
- norm_gain: float32 [8, 1024], P('section'), may hold values from 0.1 to 1.9
- query_weight: bfloat16 [8, 1024, 16384], P('section', None, 'head'), as said below
- key_weight: bfloat16 [8, 1024, 16384], P('section', None, 'head'), may hold values from -0.1875 to 0.1875
- value_weight: bfloat16 [8, 1024, 16384], P('section', None, 'head'), may hold values from -0.1875 to 0.1875
- out_weight: bfloat16 [8, 16384, 1024], P('section', 'head'), may hold values from -0.1875 to 0.1875
- saved_inputs: bfloat16 [8, 4, 256, 1024], P('section', None, None, 'head'), may hold values from -6 to 6
- reload_slot: int32 [2, 8], replicated, may hold values from 0 to 3
Outputs:
- next_inputs: bfloat16 [8, 256, 1024], P('section')
- next_cotangents: bfloat16 [8, 256, 1024], P('section')
- saved_after: bfloat16 [8, 4, 256, 1024], P('section', None, None, 'head')
- query_grad: bfloat16 [8, 1024, 16384], P('section', None, 'head')
- key_grad: bfloat16 [8, 1024, 16384], P('section', None, 'head')
- value_grad: bfloat16 [8, 1024, 16384], P('section', None, 'head')
- out_grad: bfloat16 [8, 16384, 1024], P('section', 'head')
- gain_grad: float32 [8, 1024], P('section', 'head')
The draws below stay inside these ranges and needn't reach their ends.
Inputs may be any that keep to these rules, and one draw needn't show every extreme that they name: `query_weight`: independent entries.
All inputs are finite; a program needn't handle non-finite values.
Results may differ from the reference program's by a relative error of at most 0.015.
The reference program's roundings to bfloat16 on the way count: a program that leaves them out, or rounds other values in their place, can miss the bound.
Values may be sent and summed in bfloat16 or wider, within the bound.
No kernel may reach another device: no remote copies, remote signals or barrier semaphores. Data moves between devices by JAX's collectives and lax.ppermute only.
A program may use at most 128 MiB of HBM per device.

```python
import math
import jax
import jax.numpy as jnp
from jax import lax

D = 1024
HEADS = 128
DK = 128
MB = 256
SLOTS = 4
TICKS = 2
SECTIONS = 8


def draw_query_weight(key, part):
    base = jax.random.normal(jax.random.fold_in(key, 11), (SECTIONS, D, HEADS * DK), jnp.float32) / math.sqrt(D)
    return base.astype(jnp.bfloat16)


def place_ends(drawn, key, low, largest):
    shape = drawn.shape
    index_at = [jax.random.randint(jax.random.fold_in(key, axis), (), 0, shape[axis]) for axis in range(len(shape))]
    drawn = drawn.at[tuple(index_at)].set(low)
    longest = shape.index(max(shape))
    index_at[longest] = (index_at[longest] + 1) % shape[longest]
    return drawn.at[tuple(index_at)].set(largest)


def block_levels(own_key, extent, pieces, least, largest):
    gain = 1.0
    for dim, blocks in pieces:
        draws = jax.random.uniform(jax.random.fold_in(jax.random.fold_in(own_key, 6), dim), (blocks,), jnp.float32, least / len(pieces), largest / len(pieces))
        gain = gain * jnp.repeat(jnp.exp(draws), extent[dim] // blocks).reshape((-1,) + (1,) * (len(extent) - 1 - dim))
    return gain


def gaussian(rng, shape, width, most, pieces=(), kind=jnp.bfloat16):
    values = width * jax.random.normal(rng, shape, jnp.float32)
    if pieces:
        values = values * block_levels(rng, shape, pieces, -0.22, 0.18)
    return jnp.clip(values, -most, most).astype(kind)


def setup_inputs(seed: int = 0) -> dict:
    arg_keys = jax.random.split(jax.random.key(seed), 12)
    section_inputs = gaussian(arg_keys[0], (SECTIONS, MB, D), 1.0, 6.0, ((0, 8),))
    section_cotangents = gaussian(arg_keys[1], (SECTIONS, MB, D), 1.0, 6.0, ((0, 8),))
    fresh_tokens = gaussian(arg_keys[2], (TICKS, MB, D), 1.0, 6.0)
    fresh_cotangents = gaussian(arg_keys[3], (TICKS, MB, D), 1.0, 6.0)
    norm_gain = jnp.clip(1.0 + 0.18 * jax.random.normal(arg_keys[4], (SECTIONS, D), jnp.float32), 0.1, 1.9)
    query_weight = draw_query_weight(jax.random.fold_in(arg_keys[11], 71), 0)
    key_weight = gaussian(arg_keys[6], (SECTIONS, D, HEADS * DK), D ** -0.5, 0.1875, ((0, 8), (2, 16)))
    value_weight = gaussian(arg_keys[7], (SECTIONS, D, HEADS * DK), D ** -0.5, 0.1875, ((0, 8), (2, 16)))
    out_weight = gaussian(arg_keys[8], (SECTIONS, HEADS * DK, D), (HEADS * DK // 16) ** -0.5, 0.1875, ((0, 8), (1, 16)))
    saved_inputs = gaussian(arg_keys[9], (SECTIONS, SLOTS, MB, D), 1.0, 6.0, ((0, 8), (3, 16)))
    reload_slot = place_ends(jax.random.randint(arg_keys[10], (TICKS, SECTIONS), 0, SLOTS), jax.random.fold_in(arg_keys[10], 1), 0, SLOTS - 1).astype(jnp.int32)
    return {"section_inputs": section_inputs, "section_cotangents": section_cotangents, "fresh_tokens": fresh_tokens, "fresh_cotangents": fresh_cotangents, "norm_gain": norm_gain, "query_weight": query_weight, "key_weight": key_weight, "value_weight": value_weight, "out_weight": out_weight, "saved_inputs": saved_inputs, "reload_slot": reload_slot}


epsilon = 1e-06

def normalize(rows, gain_row):
    floats = rows.astype(jnp.float32)
    inverse = lax.rsqrt(lax.optimization_barrier(jnp.mean(floats * floats, axis=-1, keepdims=True)) + epsilon)
    unit_rows = floats * inverse
    return ((unit_rows * gain_row).astype(jnp.bfloat16), unit_rows, inverse)

def split_heads(rows):
    return rows.reshape(rows.shape[0], -1, DK).astype(jnp.float32)

def attend(normed, query_part, key_part, value_part):
    queries = jnp.dot(normed, query_part, preferred_element_type=jnp.float32).astype(jnp.bfloat16)
    key_rows = jnp.dot(normed, key_part, preferred_element_type=jnp.float32).astype(jnp.bfloat16)
    value_rows = jnp.dot(normed, value_part, preferred_element_type=jnp.float32).astype(jnp.bfloat16)
    scores = jnp.einsum('qhd,khd->hqk', split_heads(queries), split_heads(key_rows)) * DK ** (-0.5)
    highest = lax.optimization_barrier(jnp.max(scores, axis=-1, keepdims=True))
    exponent = jnp.exp(scores - highest)
    softmax_rows = exponent / lax.optimization_barrier(jnp.sum(exponent, axis=-1, keepdims=True))
    softmax_low = softmax_rows.astype(jnp.bfloat16)
    context = jnp.einsum('hqk,khd->qhd', softmax_low.astype(jnp.float32), split_heads(value_rows))
    context = context.astype(jnp.bfloat16).reshape(normed.shape[0], -1)
    return (queries, key_rows, value_rows, softmax_rows, softmax_low, context)

def forward_layer(rows, gain_row, query_part, key_part, value_part, out_part):
    normed, unit_rows, inverse = normalize(rows, gain_row)
    context = attend(normed, query_part, key_part, value_part)[5]
    total = rows.astype(jnp.float32) + jnp.dot(context, out_part, preferred_element_type=jnp.float32)
    return total.astype(jnp.bfloat16)

def backward_layer(rows, upstream, gain_row, query_part, key_part, value_part, out_part):
    normed, unit_rows, inverse = normalize(rows, gain_row)
    queries, key_rows, value_rows, softmax_rows, softmax_low, context = attend(normed, query_part, key_part, value_part)
    token_count = rows.shape[0]
    out_term = jnp.dot(context.T, upstream, preferred_element_type=jnp.float32)
    context_grad = jnp.dot(upstream, out_part.T, preferred_element_type=jnp.float32).astype(jnp.bfloat16)
    softmax_grad = jnp.einsum('qhd,khd->hqk', split_heads(context_grad), split_heads(value_rows))
    value_rows_grad = jnp.einsum('hqk,qhd->khd', softmax_low.astype(jnp.float32), split_heads(context_grad))
    value_rows_grad = value_rows_grad.astype(jnp.bfloat16).reshape(token_count, -1)
    inner = lax.optimization_barrier(jnp.sum(softmax_rows * softmax_grad, axis=-1, keepdims=True))
    score_grad = (softmax_rows * (softmax_grad - inner) * DK ** (-0.5)).astype(jnp.bfloat16).astype(jnp.float32)
    queries_grad = jnp.einsum('hqk,khd->qhd', score_grad, split_heads(key_rows)).astype(jnp.bfloat16).reshape(token_count, -1)
    key_rows_grad = jnp.einsum('hqk,qhd->khd', score_grad, split_heads(queries)).astype(jnp.bfloat16).reshape(token_count, -1)
    query_term = jnp.dot(normed.T, queries_grad, preferred_element_type=jnp.float32)
    key_term = jnp.dot(normed.T, key_rows_grad, preferred_element_type=jnp.float32)
    value_term = jnp.dot(normed.T, value_rows_grad, preferred_element_type=jnp.float32)
    normed_grad = jnp.dot(queries_grad, query_part.T, preferred_element_type=jnp.float32)
    normed_grad = normed_grad + jnp.dot(key_rows_grad, key_part.T, preferred_element_type=jnp.float32)
    normed_grad = normed_grad + jnp.dot(value_rows_grad, value_part.T, preferred_element_type=jnp.float32)
    gain_term = lax.optimization_barrier(jnp.sum(normed_grad * unit_rows, axis=0))
    unit_grad = normed_grad * gain_row
    along = lax.optimization_barrier(jnp.mean(unit_grad * unit_rows, axis=-1, keepdims=True))
    returned = (upstream.astype(jnp.float32) + inverse * (unit_grad - unit_rows * along)).astype(jnp.bfloat16)
    return (returned, (query_term, key_term, value_term, out_term, gain_term))

def reference(section_inputs, section_cotangents, fresh_tokens, fresh_cotangents, norm_gain, query_weight, key_weight, value_weight, out_weight, saved_inputs, reload_slot):
    count = section_inputs.shape[0]
    stores = [saved_inputs[number] for number in range(count)]
    produced = [[None] * TICKS for number in range(count)]
    loaded = [[None] * TICKS for number in range(count)]
    for section_number in range(count):
        row_store = stores[count - 1 - section_number]
        for tick_number in range(TICKS):
            if tick_number == 0:
                current = section_inputs[section_number]
            elif section_number == 0:
                current = fresh_tokens[tick_number - 1]
            else:
                current = produced[section_number - 1][tick_number - 1]
            slot = reload_slot[tick_number, section_number]
            loaded[section_number][tick_number] = lax.dynamic_index_in_dim(row_store, slot, 0, keepdims=False)
            row_store = lax.dynamic_update_index_in_dim(row_store, current, slot, 0)
            produced[section_number][tick_number] = forward_layer(current, norm_gain[section_number], query_weight[section_number], key_weight[section_number], value_weight[section_number], out_weight[section_number])
        stores[count - 1 - section_number] = row_store
    returned = [[None] * TICKS for number in range(count)]
    grads = [None] * count
    for section_number in range(count - 1, -1, -1):
        sums = None
        for tick_number in range(TICKS):
            if tick_number == 0:
                upstream = section_cotangents[section_number]
            elif section_number == count - 1:
                upstream = fresh_cotangents[tick_number - 1]
            else:
                upstream = returned[section_number + 1][tick_number - 1]
            result, terms = backward_layer(loaded[section_number][tick_number], upstream, norm_gain[section_number], query_weight[section_number], key_weight[section_number], value_weight[section_number], out_weight[section_number])
            returned[section_number][tick_number] = result
            sums = terms if sums is None else tuple((a + b for a, b in zip(sums, terms)))
        grads[section_number] = sums
    next_inputs = jnp.stack([fresh_tokens[TICKS - 1]] + [produced[number - 1][TICKS - 1] for number in range(1, count)])
    next_cotangents = jnp.stack([returned[number + 1][TICKS - 1] for number in range(count - 1)] + [fresh_cotangents[TICKS - 1]])
    saved_after = jnp.stack(stores)
    query_grad = jnp.stack([grads[number][0] for number in range(count)]).astype(jnp.bfloat16)
    key_grad = jnp.stack([grads[number][1] for number in range(count)]).astype(jnp.bfloat16)
    value_grad = jnp.stack([grads[number][2] for number in range(count)]).astype(jnp.bfloat16)
    out_grad = jnp.stack([grads[number][3] for number in range(count)]).astype(jnp.bfloat16)
    gain_grad = jnp.stack([grads[number][4] for number in range(count)])
    return (next_inputs, next_cotangents, saved_after, query_grad, key_grad, value_grad, out_grad, gain_grad)
```

```python
import jax
import jax.numpy as jnp
from jax import lax
from jax.experimental import pallas as pl
from jax.experimental.pallas import tpu as pltpu
from jax.sharding import PartitionSpec as P

DK = 128
TICKS = 2
SCALE = DK ** (-0.5)
EPSILON = 1e-06
BF16 = jnp.bfloat16
F32 = jnp.float32
NT = (((1,), (1,)), ((), ()))
TN = (((0,), (0,)), ((), ()))
PAIR = 2 * DK
MIB = 1024 * 1024


def dot(a, b):
    return jnp.dot(a, b, preferred_element_type=F32)


def dot_nt(a, b):
    return lax.dot_general(a, b, NT, preferred_element_type=F32)


def dot_tn(a, b):
    return lax.dot_general(a, b, TN, preferred_element_type=F32)


def normalize(rows, gain_row):
    floats = rows.astype(F32)
    inverse = lax.rsqrt(jnp.mean(floats * floats, axis=-1, keepdims=True) + EPSILON)
    unit_rows = floats * inverse
    return unit_rows * gain_row, unit_rows, inverse


def softmax(queries, key_rows):
    scores = dot_nt(queries, key_rows) * SCALE
    exponent = jnp.exp(scores - jnp.max(scores, axis=-1, keepdims=True))
    return exponent * (1.0 / jnp.sum(exponent, axis=-1, keepdims=True))


def split_out(core, total, keep_ref, send_ref):
    half = keep_ref.shape[0]
    keep_ref[...] = total[pl.ds(pl.multiple_of(core * half, half), half), :]
    send_ref[...] = total[pl.ds(pl.multiple_of((1 - core) * half, half), half), :].astype(BF16)


def forward_kernel(core_ref, rows_ref, gain_ref, wq, wk, wv, wo, keep_ref, send_ref, normed, total):
    step = pl.program_id(0)

    @pl.when(step == 0)
    def _():
        normed[...] = normalize(rows_ref[...], gain_ref[...])[0].astype(BF16)
        total[...] = jnp.zeros_like(total)

    n = normed[...]
    queries = dot(n, wq[...]).astype(BF16)
    key_rows = dot(n, wk[...]).astype(BF16)
    value_rows = dot(n, wv[...]).astype(BF16)
    parts = []
    for i in range(2):
        at = slice(i * DK, (i + 1) * DK)
        low = softmax(queries[:, at], key_rows[:, at]).astype(BF16)
        parts.append(dot(low, value_rows[:, at]).astype(BF16))
    total[...] += dot(jnp.concatenate(parts, axis=1), wo[...])

    @pl.when(step == pl.num_programs(0) - 1)
    def _():
        split_out(core_ref[0], total, keep_ref, send_ref)


def whole(shape):
    return pl.BlockSpec(shape, lambda i: (0,) * len(shape))


def columns(rows):
    return pl.BlockSpec((rows, PAIR), lambda i: (0, i))


def rows_of(cols):
    return pl.BlockSpec((PAIR, cols), lambda i: (i, 0))


SMEM = pl.BlockSpec(memory_space=pltpu.SMEM)


def params(limit):
    return pltpu.CompilerParams(
        dimension_semantics=("arbitrary",), vmem_limit_bytes=limit * MIB
    )


def forward_partial(core, rows, gain, wq, wk, wv, wo):
    tokens, width = rows.shape
    inner = wq.shape[1]
    return pl.pallas_call(
        forward_kernel,
        grid=(inner // PAIR,),
        in_specs=[SMEM, whole((tokens, width)), whole((1, width))]
        + [columns(width)] * 3
        + [rows_of(width)],
        out_specs=[whole((tokens // 2, width))] * 2,
        out_shape=[
            jax.ShapeDtypeStruct((tokens // 2, width), F32),
            jax.ShapeDtypeStruct((tokens // 2, width), BF16),
        ],
        scratch_shapes=[pltpu.VMEM((tokens, width), BF16), pltpu.VMEM((tokens, width), F32)],
        compiler_params=params(24),
        cost_estimate=pl.CostEstimate(
            flops=8 * tokens * width * inner, bytes_accessed=8 * width * inner, transcendentals=0
        ),
        name="forward_part",
    )(core, rows, gain, wq, wk, wv, wo)


def recompute_kernel(
    place_ref, mine_ref, other_ref, gain_ref, wq, wk, wv,
    block_ref, normed_t_ref, q_ref, k_ref, v_ref, soft_ref, context_ref, block_t, normed,
):
    step = pl.program_id(0)

    @pl.when(step == 0)
    def _():
        core, high, column = place_ref[0], place_ref[1], place_ref[2]
        share = mine_ref.shape[1]
        for j in range(4):
            for i in range(2):
                head = (column ^ j) * 4 + (high ^ i) * 2
                for ref, c in ((mine_ref, core), (other_ref, 1 - core)):
                    at = pl.multiple_of((head + c) * share, share)
                    block_t[pl.ds(at, share), :] = ref[2 * j + i]
        block = block_t[...].T
        block_ref[...] = block
        n = normalize(block, gain_ref[...])[0].astype(BF16)
        normed[...] = n
        normed_t_ref[...] = n.T

    n = normed[...]
    queries = dot(n, wq[...]).astype(BF16)
    key_rows = dot(n, wk[...]).astype(BF16)
    value_rows = dot(n, wv[...]).astype(BF16)
    q_ref[...] = queries
    k_ref[...] = key_rows
    v_ref[...] = value_rows
    for i in range(2):
        at = slice(i * DK, (i + 1) * DK)
        rows = softmax(queries[:, at], key_rows[:, at])
        soft_ref[i] = rows
        context_ref[:, at] = dot(rows.astype(BF16), value_rows[:, at]).astype(BF16)


def recompute(place, mine, other, gain, wq, wk, wv):
    pieces, share, tokens = mine.shape
    width, inner = wq.shape
    heads = inner // DK
    flat = jax.ShapeDtypeStruct((tokens, inner), BF16)
    return pl.pallas_call(
        recompute_kernel,
        grid=(inner // PAIR,),
        in_specs=[SMEM, whole(mine.shape), whole(mine.shape), whole((1, width))]
        + [columns(width)] * 3,
        out_specs=[
            whole((tokens, width)),
            whole((width, tokens)),
            columns(tokens),
            columns(tokens),
            columns(tokens),
            pl.BlockSpec((2, tokens, tokens), lambda i: (i, 0, 0)),
            columns(tokens),
        ],
        out_shape=[
            jax.ShapeDtypeStruct((tokens, width), BF16),
            jax.ShapeDtypeStruct((width, tokens), BF16),
            flat,
            flat,
            flat,
            jax.ShapeDtypeStruct((heads, tokens, tokens), F32),
            flat,
        ],
        scratch_shapes=[pltpu.VMEM((width, tokens), BF16), pltpu.VMEM((tokens, width), BF16)],
        compiler_params=params(24),
        cost_estimate=pl.CostEstimate(
            flops=7 * tokens * width * inner, bytes_accessed=6 * width * inner, transcendentals=0
        ),
        name="recompute_part",
    )(place, mine, other, gain, wq, wk, wv)


def backward_kernel(
    core_ref, g_ref, q_ref, k_ref, v_ref, soft_ref, wq, wk, wv, wo,
    keep_ref, send_ref, qg_ref, kg_ref, vg_ref, total,
):
    step = pl.program_id(0)

    @pl.when(step == 0)
    def _():
        total[...] = jnp.zeros_like(total)

    grads = dot_nt(g_ref[...], wo[...]).astype(BF16)
    for i in range(2):
        at = slice(i * DK, (i + 1) * DK)
        rows = soft_ref[i]
        grad = grads[:, at]
        soft_grad = dot_nt(grad, v_ref[:, at])
        vg_ref[:, at] = dot_tn(rows.astype(BF16), grad).astype(BF16)
        along = jnp.sum(rows * soft_grad, axis=-1, keepdims=True)
        score_grad = (rows * (soft_grad - along) * SCALE).astype(BF16)
        qg_ref[:, at] = dot(score_grad, k_ref[:, at]).astype(BF16)
        kg_ref[:, at] = dot_tn(score_grad, q_ref[:, at]).astype(BF16)
    total[...] += (
        dot_nt(qg_ref[...], wq[...]) + dot_nt(kg_ref[...], wk[...]) + dot_nt(vg_ref[...], wv[...])
    )

    @pl.when(step == pl.num_programs(0) - 1)
    def _():
        split_out(core_ref[0], total, keep_ref, send_ref)


def backward_partial(core, g, q, k, v, soft, wq, wk, wv, wo):
    tokens, width = g.shape
    inner = wq.shape[1]
    flat = jax.ShapeDtypeStruct((tokens, inner), BF16)
    return pl.pallas_call(
        backward_kernel,
        grid=(inner // PAIR,),
        in_specs=[SMEM, whole((tokens, width))]
        + [columns(tokens)] * 3
        + [pl.BlockSpec((2, tokens, tokens), lambda i: (i, 0, 0))]
        + [columns(width)] * 3
        + [rows_of(width)],
        out_specs=[whole((tokens // 2, width))] * 2 + [columns(tokens)] * 3,
        out_shape=[
            jax.ShapeDtypeStruct((tokens // 2, width), F32),
            jax.ShapeDtypeStruct((tokens // 2, width), BF16),
            flat,
            flat,
            flat,
        ],
        scratch_shapes=[pltpu.VMEM((tokens, width), F32)],
        compiler_params=params(24),
        cost_estimate=pl.CostEstimate(
            flops=9 * tokens * width * inner, bytes_accessed=10 * width * inner, transcendentals=0
        ),
        name="backward_part",
    )(core, g, q, k, v, soft, wq, wk, wv, wo)


def weight_kernel(n0, n1, q0, q1, k0, k1, v0, v1, c0, c1, g0, g1, dq, dk, dv, do):
    for a0, a1, out in ((q0, q1, dq), (k0, k1, dk), (v0, v1, dv)):
        out[...] = (dot(n0[...], a0[...]) + dot(n1[...], a1[...])).astype(BF16)
    do[...] = (dot_tn(c0[...], g0[...]) + dot_tn(c1[...], g1[...])).astype(BF16)


def weight_grads(normed_t, q, k, v, context, g):
    width, tokens = normed_t[0].shape
    inner = q[0].shape[1]
    flat = jax.ShapeDtypeStruct((width, inner), BF16)
    return pl.pallas_call(
        weight_kernel,
        grid=(inner // PAIR,),
        in_specs=[whole((width, tokens))] * 2 + [columns(tokens)] * 8 + [whole((tokens, width))] * 2,
        out_specs=[columns(width)] * 3 + [rows_of(width)],
        out_shape=[flat, flat, flat, jax.ShapeDtypeStruct((inner, width), BF16)],
        compiler_params=params(24),
        cost_estimate=pl.CostEstimate(
            flops=16 * tokens * width * inner, bytes_accessed=8 * width * inner, transcendentals=0
        ),
        name="weight_part",
    )(*normed_t, *q, *k, *v, *context, *g)


class Moves:
    def __init__(self, sections, heads):
        self.sections, self.heads = sections, heads

    def send(self, value, to):
        pairs = []
        for s in range(self.sections):
            for h in range(self.heads):
                t, k = to(s, h)
                if 0 <= t < self.sections:
                    pairs.append((s * self.heads + h, t * self.heads + k))
        return lax.ppermute(value, ("section", "head"), pairs)

    def flip(self, value, mask):
        return self.send(value, lambda s, h: (s, h ^ mask))

    def shift(self, value, by, mask):
        return self.send(value, lambda s, h: (s + by, h ^ mask))

    def mirror(self, value, mask):
        return self.send(value, lambda s, h: (self.sections - 1 - s, h ^ mask))


def ordered(pieces, column):
    p = list(pieces)
    low, high = (column & 1) == 1, (column & 2) == 2
    p = [jnp.where(low, p[j ^ 1], p[j]) for j in range(4)]
    p = [jnp.where(high, p[j ^ 2], p[j]) for j in range(4)]
    return jnp.concatenate(p, axis=0)


def per_device(
    section_inputs, section_cotangents, fresh_tokens, fresh_cotangents, norm_gain,
    query_weight, key_weight, value_weight, out_weight, saved_inputs, reload_slot,
):
    sections, heads = lax.axis_size("section"), lax.axis_size("head")
    section, head = lax.axis_index("section"), lax.axis_index("head")
    moves = Moves(sections, heads)
    core, high, column = head & 1, (head >> 1) & 1, head >> 2
    mirror = sections - 1 - section
    share = saved_inputs.shape[3]
    core_at = core.astype(jnp.int32)[None]
    place = jnp.stack([core, high, column]).astype(jnp.int32)
    gain = norm_gain
    wq, wk, wv, wo = query_weight[0], key_weight[0], value_weight[0], out_weight[0]
    store = jnp.swapaxes(saved_inputs[0], 1, 2)
    tokens, width = section_inputs.shape[1:]
    rows = tokens // 8
    row_at = core * (tokens // 2) + column * rows

    def share_of(block):
        return lax.dynamic_slice_in_dim(block, head * share, share, 1).T

    def take_rows(block):
        return lax.dynamic_slice_in_dim(block, row_at, rows, 0)

    def scatter_sum(keep, send):
        got = moves.flip(send, 1)
        mine = keep + got.astype(F32)
        low = mine.astype(BF16)
        parts = []
        for j in (1, 2, 3):
            piece = lax.dynamic_slice_in_dim(low, (column ^ j) * rows, rows, 0)
            parts.append(moves.flip(piece, 4 * j))
        own = lax.dynamic_slice_in_dim(mine, column * rows, rows, 0)
        return own + (parts[0].astype(F32) + (parts[1].astype(F32) + parts[2].astype(F32)))

    def pass_on(value, by):
        low = value.astype(BF16)
        first = moves.shift(low, by, 0)
        second = moves.shift(low, by, 2)
        return (first.astype(F32) + second.astype(F32)).astype(BF16)

    def gather_rows(piece):
        pieces = [piece] + [moves.flip(piece, 4 * j) for j in (1, 2, 3)]
        mine = ordered(pieces, column)
        other = moves.flip(mine, 1)
        return jnp.concatenate(
            [jnp.where(core == 0, mine, other), jnp.where(core == 0, other, mine)], axis=0
        )

    def gather_shares(mine, far):
        both = jnp.stack([mine, far])
        pieces = [both] + [moves.flip(both, 4 * j) for j in (1, 2, 3)]
        mine = jnp.concatenate(pieces, axis=0)
        return mine, moves.flip(mine, 1)

    slot_here = [lax.dynamic_index_in_dim(reload_slot[t], section, 0, keepdims=False) for t in range(TICKS)]
    slot_there = [lax.dynamic_index_in_dim(reload_slot[t], mirror, 0, keepdims=False) for t in range(TICKS)]
    current, upstream = section_inputs[0], section_cotangents[0]

    held = [lax.dynamic_index_in_dim(store, slot_there[t], 0, keepdims=False) for t in range(TICKS)]
    same = slot_here[0] == slot_here[1]
    own_first = share_of(current)
    going = jnp.stack([held[0], held[1], own_first])
    near = moves.mirror(going, 0)
    far_first = moves.mirror(going[:2], 2)
    pair_first = moves.flip(own_first, 2)
    store = lax.dynamic_update_index_in_dim(store, near[2], slot_there[0], 0)
    reload = [
        gather_shares(near[0], far_first[0]),
        gather_shares(
            jnp.where(same, own_first, near[1]), jnp.where(same, pair_first, far_first[1])
        ),
    ]

    contexts, normed_ts, qgs, kgs, vgs, gs = [], [], [], [], [], []
    gain_sum = 0.0
    for t in range(TICKS):
        keep, send = forward_partial(core_at, current, gain, wq, wk, wv, wo)
        block, normed_t, q, k, v, soft, context = recompute(place, *reload[t], gain, wq, wk, wv)
        back_keep, back_send, qg, kg, vg = backward_partial(
            core_at, upstream, q, k, v, soft, wq, wk, wv, wo
        )
        contexts.append(context)
        normed_ts.append(normed_t)
        qgs.append(qg)
        kgs.append(kg)
        vgs.append(vg)
        gs.append(upstream)

        ahead = scatter_sum(keep, send)
        ahead = ahead + jnp.where(high == 0, take_rows(current).astype(F32), 0.0)
        ahead = pass_on(ahead, 1)
        ahead = jnp.where(section == 0, take_rows(fresh_tokens[t]), ahead)
        current = gather_rows(ahead)

        normed_grad = scatter_sum(back_keep, back_send)
        _, unit, inverse = normalize(take_rows(block), gain)
        gain_sum = gain_sum + jnp.sum(normed_grad * unit, axis=0)
        unit_grad = normed_grad * gain
        along = jnp.mean(unit_grad * unit, axis=-1, keepdims=True)
        back = jnp.where(high == 0, take_rows(upstream).astype(F32), 0.0)
        back = back + inverse * (unit_grad - unit * along)
        back = pass_on(back, -1)
        back = jnp.where(section == sections - 1, take_rows(fresh_cotangents[t]), back)
        upstream = gather_rows(back)
        if t == 0:
            arrived = moves.mirror(share_of(current), 0)
            store = lax.dynamic_update_index_in_dim(store, arrived, slot_there[1], 0)

    grads = weight_grads(normed_ts, qgs, kgs, vgs, contexts, gs)
    gain_grad = jnp.sum(lax.all_to_all(gain_sum.reshape(heads, share), "head", 0, 0), axis=0)
    return (
        current[None],
        upstream[None],
        jnp.swapaxes(store, 1, 2)[None],
        grads[0][None],
        grads[1][None],
        grads[2][None],
        grads[3][None],
        gain_grad[None],
    )


def solution(mesh):
    placed = (
        P("section", None, None),
        P("section", None, None),
        P(),
        P(),
        P("section", None),
        P("section", None, "head"),
        P("section", None, "head"),
        P("section", None, "head"),
        P("section", "head", None),
        P("section", None, None, "head"),
        P(),
    )
    return jax.shard_map(
        per_device,
        mesh=mesh,
        in_specs=placed,
        out_specs=(
            P("section", None, None),
            P("section", None, None),
            P("section", None, None, "head"),
            P("section", None, "head"),
            P("section", None, "head"),
            P("section", None, "head"),
            P("section", "head", None),
            P("section", "head"),
        ),
        check_vma=False,
    )
```

```python
import jax
import jax.numpy as jnp
from jax import lax
from jax.experimental import pallas as pl
from jax.experimental.pallas import tpu as pltpu
from jax.sharding import PartitionSpec as P

DK = 128
TICKS = 2
SCALE = DK ** (-0.5)
EPSILON = 1e-06
BF16 = jnp.bfloat16
F32 = jnp.float32
NT = (((1,), (1,)), ((), ()))
TN = (((0,), (0,)), ((), ()))
MIB = 1024 * 1024


def dot(a, b):
    return jnp.dot(a, b, preferred_element_type=F32)


def dot_nt(a, b):
    return lax.dot_general(a, b, NT, preferred_element_type=F32)


def dot_tn(a, b):
    return lax.dot_general(a, b, TN, preferred_element_type=F32)


def normalize(rows, gain_row):
    floats = rows.astype(F32)
    inverse = lax.rsqrt(jnp.mean(floats * floats, axis=-1, keepdims=True) + EPSILON)
    unit_rows = floats * inverse
    return unit_rows * gain_row, unit_rows, inverse


def softmax(queries, key_rows):
    scores = dot_nt(queries, key_rows) * SCALE
    exponent = jnp.exp(scores - jnp.max(scores, axis=-1, keepdims=True))
    return exponent * (1.0 / jnp.sum(exponent, axis=-1, keepdims=True))


VMEM = pl.BlockSpec(memory_space=pltpu.VMEM)
SMEM = pl.BlockSpec(memory_space=pltpu.SMEM)
ANYWHERE = pl.BlockSpec(memory_space=pltpu.HBM)


def shape(dtype, *dims):
    return jax.ShapeDtypeStruct(dims, dtype)


def kept(dtype, *dims):
    return pltpu.VMEM(dims, dtype)


def in_hbm(dtype, *dims):
    return pltpu.HBM(dims, dtype)


def from_hbm(value):
    return pltpu.with_memory_space_constraint(value, pltpu.HBM)


def where_am_i():
    head = lax.axis_index("head")
    return head & 1, (head >> 1) & 1, head >> 2, lax.axis_index("section")


def kernel_call(body, name, args, outs, scratch=(), scalars=0, loose=0, flops=0, limit=16):
    moved = sum(a.size * a.dtype.itemsize for a in args)
    return pl.pallas_call(
        body,
        in_specs=[SMEM] * scalars + [VMEM] * (len(args) - scalars - loose) + [ANYWHERE] * loose,
        out_specs=[ANYWHERE if getattr(o, "memory_space", None) is pltpu.HBM else VMEM for o in outs],
        out_shape=list(outs),
        scratch_shapes=list(scratch),
        compiler_params=pltpu.CompilerParams(vmem_limit_bytes=limit * MIB),
        cost_estimate=pl.CostEstimate(flops=flops, bytes_accessed=moved, transcendentals=0),
        name=name,
    )(*args)


def lanes(i):
    return slice(i * DK, (i + 1) * DK)


def at_rows(start, count):
    return pl.ds(pl.multiple_of(start, count), count)


def run_copies(pairs, sems):
    copies = [pltpu.make_async_copy(src, dst, sems.at[i]) for i, (src, dst) in enumerate(pairs)]
    for copy in copies:
        copy.start()
    for copy in copies:
        copy.wait()


def pick_held(slots, store, out, sems):
    mirror = lax.axis_size("section") - 1 - lax.axis_index("section")
    run_copies([(store.at[slots[t, mirror]], out.at[t]) for t in range(TICKS)], sems)


def pick_rows(current, upstream, tokens, cotangents, z, *refs):
    *fresh, sems = refs
    core, _, column, _ = where_am_i()
    rows = z.shape[0] // 2
    at = at_rows(core * (current.shape[0] // 2) + column * rows, rows)
    pairs = [(current.at[at, :], z.at[:rows, :]), (upstream.at[at, :], z.at[rows:, :])]
    for t in range(TICKS):
        pairs.append((tokens.at[t, at, :], fresh[t].at[:rows, :]))
        pairs.append((cotangents.at[t, at, :], fresh[t].at[rows:, :]))
    run_copies(pairs, sems)


def turn_first(slots, current, shares, flag, turned):
    section, head = lax.axis_index("section"), lax.axis_index("head")
    share = shares.shape[1]
    turned[...] = current[...].T
    shares[0] = turned[at_rows(head * share, share), :]
    shares[1] = turned[at_rows((head ^ 2) * share, share), :]
    same = jnp.where(slots[0, section] == slots[1, section], 1.0, 0.0)
    flag[...] = jnp.full(flag.shape, same, F32)


def pick_reload(near, far, shares, flag, both):
    both[0] = near[0]
    both[1] = far[0]
    same = flag[0:1, :] > 0.5
    for y, ref in enumerate((near, far)):
        both[2 + y] = jnp.where(same, shares[y].astype(F32), ref[1].astype(F32)).astype(BF16)


def part_reload(own, got1, got2, got3, after, first, second):
    for j, ref in enumerate((own, got1, got2, got3)):
        first[2 * j : 2 * j + 2] = ref[0:2]
        second[2 * j : 2 * j + 2] = ref[2:4]


def pick_share(first_shares, current, after, out, turned):
    share = first_shares.shape[1]
    turned[...] = current[...].T
    out[0] = first_shares[0]
    out[1] = turned[at_rows(lax.axis_index("head") * share, share), :]


def put_store(slots, store, arrived, out):
    mirror = lax.axis_size("section") - 1 - lax.axis_index("section")
    out[...] = store[...]
    for t in range(TICKS):
        out[slots[t, mirror]] = arrived[t]


def attend_and_project(n, total, keep_ref, send_ref, wq, wk, wv, wo, q, k, v, context, ready):
    ready(0)
    q[...] = dot(n, wq[...]).astype(BF16)
    ready(1)
    k[...] = dot(n, wk[...]).astype(BF16)
    ready(2)
    v[...] = dot(n, wv[...]).astype(BF16)
    for i in range(q.shape[1] // DK):
        at = lanes(i)
        low = softmax(q[:, at], k[:, at]).astype(BF16)
        context[:, at] = dot(low, v[:, at]).astype(BF16)
    ready(3)
    total[...] = dot(context[...], wo[...])
    core = where_am_i()[0]
    half = keep_ref.shape[0]
    keep_ref[...] = total[at_rows(core * half, half), :]
    send_ref[...] = total[at_rows((1 - core) * half, half), :].astype(BF16)


def forward_first(rows, gain, hq, hk, hv, ho, wq, wk, wv, wo, keep, send, q, k, v, context, total, sems):
    copies = [
        pltpu.make_async_copy(src, dst, sems.at[i])
        for i, (src, dst) in enumerate(((hq, wq), (hk, wk), (hv, wv), (ho, wo)))
    ]
    for copy in copies:
        copy.start()
    n = normalize(rows[...], gain[...])[0].astype(BF16)
    attend_and_project(
        n, total, keep, send, wq, wk, wv, wo, q, k, v, context, lambda i: copies[i].wait()
    )


def put_pieces(pieces, first, second):
    core, _, column, _ = where_am_i()
    rows = pieces[0].shape[0] // 2
    half = first.shape[0] // 2
    for i, ref in enumerate(pieces):
        c = core if i < 4 else 1 - core
        at = at_rows(c * half + (column ^ (i % 4)) * rows, rows)
        first[at, :] = ref[:rows, :]
        second[at, :] = ref[rows:, :]


def forward_next(gain, wq, wk, wv, wo, *refs):
    pieces, (rows, g, keep, send), (q, k, v, context, total) = refs[:8], refs[8:12], refs[12:]
    put_pieces(pieces, rows, g)
    n = normalize(rows[...], gain[...])[0].astype(BF16)
    attend_and_project(n, total, keep, send, wq, wk, wv, wo, q, k, v, context, lambda i: None)


def put_last(gain_rows, gain_other, *refs):
    pieces, (rows, g, gain_out) = refs[:8], refs[8:]
    put_pieces(pieces, rows, g)
    value = get_gain(gain_rows, 0) + get_gain(gain_other, 0)
    share = gain_out.shape[1]
    for h in range(value.shape[1] // share):

        @pl.when(lax.axis_index("head") == h)
        def _():
            gain_out[...] = value[:, h * share : (h + 1) * share]


def recompute_kernel(gain, wq, wk, wv, *refs):
    mine, other, block_ref, normed_out, q, k, v, soft, context_out = refs[:9]
    block_t, normed_t, context, sems = refs[-4:]
    core, high, column, _ = where_am_i()
    share = mine.shape[1]
    for ref, c in ((mine, core), (other, 1 - core)):
        for i in range(8):
            head = (column ^ (i // 2)) * 4 + (high ^ (i % 2)) * 2 + c
            block_t[at_rows(head * share, share), :] = ref[i]
    block = block_t[...].T
    block_ref[...] = block
    n = normalize(block, gain[...])[0].astype(BF16)
    normed_t[...] = n.T
    first = pltpu.make_async_copy(normed_t, normed_out, sems.at[0])
    first.start()
    q[...] = dot(n, wq[...]).astype(BF16)
    k[...] = dot(n, wk[...]).astype(BF16)
    v[...] = dot(n, wv[...]).astype(BF16)
    for i in range(q.shape[1] // DK):
        at = lanes(i)
        rows = softmax(q[:, at], k[:, at])
        soft[i] = rows
        context[:, at] = dot(rows.astype(BF16), v[:, at]).astype(BF16)
    second = pltpu.make_async_copy(context, context_out, sems.at[1])
    second.start()
    first.wait()
    second.wait()


def backward_kernel(
    g, block, gain, q, k, v, soft, wq, wk, wv, wo, ahead_keep, ahead_send, gain_before,
    *refs,
):
    keep, send, qg_out, kg_out, vg_out, gain_part, qg, kg, vg, grads, total, sems = refs[-12:]
    grads[...] = dot_nt(g[...], wo[...]).astype(BF16)
    for i in range(q.shape[1] // DK):
        at = lanes(i)
        rows = soft[i]
        grad = grads[:, at]
        soft_grad = dot_nt(grad, v[:, at])
        vg[:, at] = dot_tn(rows.astype(BF16), grad).astype(BF16)
        along = jnp.sum(rows * soft_grad, axis=-1, keepdims=True)
        score_grad = (rows * (soft_grad - along) * SCALE).astype(BF16)
        qg[:, at] = dot(score_grad, k[:, at]).astype(BF16)
        kg[:, at] = dot_tn(score_grad, q[:, at]).astype(BF16)
    copies = [
        pltpu.make_async_copy(src, dst, sems.at[i])
        for i, (src, dst) in enumerate(((qg, qg_out), (kg, kg_out), (vg, vg_out)))
    ]
    for copy in copies:
        copy.start()
    total[...] = dot_nt(qg[...], wq[...])
    total[...] += dot_nt(kg[...], wk[...])
    total[...] += dot_nt(vg[...], wv[...])
    half = ahead_keep.shape[0]
    core = where_am_i()[0]
    keep[:half, :] = ahead_keep[...]
    keep[half:, :] = total[at_rows(core * half, half), :]
    send[:half, :] = ahead_send[...]
    send[half : 2 * half, :] = total[at_rows((1 - core) * half, half), :].astype(BF16)
    unit = normalize(block[...], gain[...])[1]
    part = gain_before[...] + jnp.sum(total[...] * unit, axis=0, keepdims=True)
    gain_part[...] = part
    if send.shape[0] > 2 * half:
        put_gain(send, 2 * half, part)
    for copy in copies:
        copy.wait()


def put_gain(ref, row, value):
    value = jnp.broadcast_to(value, (16, value.shape[1]))
    high = value.astype(BF16)
    low = (value - high.astype(F32)).astype(BF16)
    is_first = lax.broadcasted_iota(jnp.int32, value.shape, 0) == 0
    ref[row : row + 16, :] = jnp.where(is_first, high.astype(F32), low.astype(F32)).astype(BF16)


def get_gain(ref, row):
    tile = ref[row : row + 16, :].astype(F32)
    return tile[0:1] + tile[1:2]


def after_core(keep, got, gain_part, *refs):
    own, to1, to2, to3, gain_out, mine = refs[-6:]
    column = where_am_i()[2]
    half = keep.shape[0] // 2
    rows = half // 4
    mine[...] = keep[...] + got[: 2 * half, :].astype(F32)
    for j, ref in ((0, own), (1, to1), (2, to2), (3, to3)):
        for part in range(2):
            at = at_rows(part * half + (column ^ j) * rows, rows)
            ref[part * rows : (part + 1) * rows, :] = mine[at, :].astype(ref.dtype)
    if got.shape[0] > 2 * half:
        value = gain_part[...] + get_gain(got, 2 * half)
        gain_out[...] = value
        for ref in (to1, to2, to3):
            put_gain(ref, 2 * rows, value)
    else:
        gain_out[...] = gain_part[...]


def after_column(own, z, block, gain, gain_part, got1, got2, got3, *refs):
    even, odd, gain_out = refs[-3:]
    core, high, column, section = where_am_i()
    rows = z.shape[0] // 2
    tokens = block.shape[0]
    total = [None, None]
    for part in range(2):
        at = slice(part * rows, (part + 1) * rows)
        total[part] = own[at, :] + (
            got1[at, :].astype(F32) + (got2[at, :].astype(F32) + got3[at, :].astype(F32))
        )
    here = jnp.where(high == 0, 1.0, 0.0).astype(F32)
    ahead = (here * z[:rows, :].astype(F32) + total[0]).astype(BF16)
    at = at_rows(core * (tokens // 2) + column * rows, rows)
    _, unit, inverse = normalize(block[at, :], gain[...])
    unit_grad = total[1] * gain[...]
    along = jnp.mean(unit_grad * unit, axis=-1, keepdims=True)
    back = here * z[rows:, :].astype(F32) + inverse * (unit_grad - unit * along)
    back = back.astype(BF16)

    @pl.when((section & 1) == 0)
    def _():
        even[...] = ahead
        odd[...] = back

    @pl.when((section & 1) == 1)
    def _():
        even[...] = back
        odd[...] = ahead

    if got1.shape[0] > 2 * rows:
        value = get_gain(got1, 2 * rows) + get_gain(got2, 2 * rows) + get_gain(got3, 2 * rows)
        put_gain(gain_out, 0, gain_part[...] + value)
    else:
        put_gain(gain_out, 0, gain_part[...])


def after_shift(even0, even1, odd0, odd1, fresh, z):
    section = where_am_i()[3]
    rows = even0.shape[0]
    even = (even0[...].astype(F32) + even1[...].astype(F32)).astype(BF16)
    odd = (odd0[...].astype(F32) + odd1[...].astype(F32)).astype(BF16)

    @pl.when((section & 1) == 0)
    def _():
        z[:rows, :] = odd
        z[rows:, :] = even

    @pl.when((section & 1) == 1)
    def _():
        z[:rows, :] = even
        z[rows:, :] = odd

    @pl.when(section == 0)
    def _():
        z[:rows, :] = fresh[:rows, :]

    @pl.when(section == lax.axis_size("section") - 1)
    def _():
        z[rows:, :] = fresh[rows:, :]


def query_key_kernel(after, n0, n1, q0, q1, k0, k1, dq, dk):
    dq[...] = (dot(n0[...], q0[...]) + dot(n1[...], q1[...])).astype(BF16)
    dk[...] = (dot(n0[...], k0[...]) + dot(n1[...], k1[...])).astype(BF16)


def value_out_kernel(after, n0, n1, v0, v1, c0, c1, g0, g1, dv, do):
    dv[...] = (dot(n0[...], v0[...]) + dot(n1[...], v1[...])).astype(BF16)
    do[...] = (dot_tn(c0[...], g0[...]) + dot_tn(c1[...], g1[...])).astype(BF16)


def weight_grads(body, name, after, normed_t, blocked, fixed, by_rows):
    steps = 4
    width, tokens = normed_t[0].shape
    inner = blocked[0].shape[1]
    block = inner // steps
    args = [after, *normed_t, *blocked, *fixed]
    outs = [pl.BlockSpec((width, block), lambda i: (0, i))] * 2
    shapes = [shape(BF16, width, inner)] * 2
    if by_rows:
        outs[1] = pl.BlockSpec((block, width), lambda i: (i, 0))
        shapes[1] = shape(BF16, inner, width)
    return pl.pallas_call(
        body,
        grid=(steps,),
        in_specs=[pl.BlockSpec(memory_space=pl.ANY)]
        + [pl.BlockSpec((width, tokens), lambda i: (0, 0))] * 2
        + [pl.BlockSpec((tokens, block), lambda i: (0, i))] * len(blocked)
        + [pl.BlockSpec((tokens, width), lambda i: (0, 0))] * len(fixed),
        out_specs=outs,
        out_shape=shapes,
        compiler_params=pltpu.CompilerParams(
            dimension_semantics=("arbitrary",), vmem_limit_bytes=16 * MIB
        ),
        cost_estimate=pl.CostEstimate(
            flops=8 * tokens * width * inner, bytes_accessed=4 * width * inner, transcendentals=0
        ),
        name=name,
    )(*args)


class Moves:
    def __init__(self, sections, heads):
        self.sections, self.heads = sections, heads

    def send(self, value, to, mask):
        pairs = []
        for s in range(self.sections):
            t = to(s)
            if 0 <= t < self.sections:
                pairs += [(s * self.heads + h, t * self.heads + (h ^ mask)) for h in range(self.heads)]
        return lax.ppermute(value, ("section", "head"), pairs)

    def flip(self, value, mask):
        return self.send(value, lambda s: s, mask)

    def even(self, value, mask):
        return self.send(value, lambda s: s ^ 1, mask)

    def odd(self, value, mask):
        return self.send(value, lambda s: ((s - 1) ^ 1) + 1, mask)

    def mirror(self, value, mask):
        return self.send(value, lambda s: self.sections - 1 - s, mask)


def per_device(
    section_inputs, section_cotangents, fresh_tokens, fresh_cotangents, norm_gain,
    query_weight, key_weight, value_weight, out_weight, saved_inputs, reload_slot,
):
    sections, heads = lax.axis_size("section"), lax.axis_size("head")
    section, head = lax.axis_index("section"), lax.axis_index("head")
    moves = Moves(sections, heads)
    share = saved_inputs.shape[3]
    gain = norm_gain
    store = jnp.swapaxes(saved_inputs[0], 1, 2)
    tokens, width = section_inputs.shape[1:]
    inner = query_weight.shape[2]
    half, rows = tokens // 2, tokens // 8
    unit_flops = 2 * tokens * width * inner
    current, upstream = section_inputs[0], section_cotangents[0]

    (going,) = kernel_call(
        pick_held, "pick_held", (reload_slot, from_hbm(store)), [kept(BF16, TICKS, share, tokens)],
        [pltpu.SemaphoreType.DMA((TICKS,))], 1, 1,
    )
    near, far = moves.mirror(going, 0), moves.mirror(going, 2)
    z, *fresh = kernel_call(
        pick_rows, "pick_rows",
        [from_hbm(a) for a in (current, upstream, fresh_tokens, fresh_cotangents)],
        [kept(BF16, 2 * rows, width)] * (1 + TICKS),
        [pltpu.SemaphoreType.DMA((2 + 2 * TICKS,))], 0, 4,
    )
    first_shares, flag = kernel_call(
        turn_first, "turn_first", (reload_slot, current),
        [kept(BF16, 2, share, tokens), kept(F32, 8, tokens)],
        [pltpu.VMEM((width, tokens), BF16)], 1,
    )
    (both,) = kernel_call(
        pick_reload, "pick_reload", (near, far, first_shares, flag),
        [kept(BF16, 2 * TICKS, share, tokens)],
    )
    arriving = [both] + [moves.flip(both, 4 * j) for j in (1, 2, 3)]

    flat = kept(BF16, tokens, inner)
    whole = kept(BF16, tokens, width)
    half_outs = [kept(F32, half, width), kept(BF16, half, width)]
    work = [pltpu.VMEM((tokens, inner), BF16)] * 4 + [pltpu.VMEM((tokens, width), F32)]
    gain_part = jnp.zeros((1, width), F32)
    left, context, grads_of, cotangents = [], [], [], []
    pieces = None

    def recompute(u):
        return kernel_call(
            recompute_kernel, "recompute", (gain, wq, wk, wv, *reload[u]),
            [
                whole, kept(BF16, width, tokens), flat, flat, flat,
                kept(F32, inner // DK, tokens, tokens), flat,
            ],
            [
                pltpu.VMEM((width, tokens), BF16), pltpu.VMEM((width, tokens), BF16),
                pltpu.VMEM((tokens, inner), BF16), pltpu.SemaphoreType.DMA((2,)),
            ], 0, 0, 5 * unit_flops,
        )

    for t in range(TICKS):
        if t == 0:
            raw = [
                from_hbm(w[0]) for w in (query_weight, key_weight, value_weight, out_weight)
            ]
            *weights, keep, send = kernel_call(
                forward_first, "forward_first", (current, gain, *raw),
                [kept(BF16, *w.shape) for w in raw] + half_outs,
                work + [pltpu.SemaphoreType.DMA((4,))], 0, 4, 5 * unit_flops,
            )
            wq, wk, wv, wo = weights
            own_shares = kernel_call(
                part_reload, "part_reload", (*arriving, send),
                [kept(BF16, 8, share, tokens)] * TICKS, (), 0, 1,
            )
            reload = [(a, moves.flip(a, 1)) for a in own_shares]
        else:
            current, upstream, keep, send = kernel_call(
                forward_next, "forward_next", (gain, wq, wk, wv, wo, *pieces),
                [whole] * 2 + half_outs, work, 0, 0, 5 * unit_flops,
            )
        if t == 0:
            read = [recompute(u) for u in range(1)]
        block, normed_t, q, k, v, soft, ctx = read[t]
        extra = 16 if t == TICKS - 1 else 0
        keep, send, qg, kg, vg, gain_part = kernel_call(
            backward_kernel, "backward",
            (upstream, block, gain, q, k, v, soft, wq, wk, wv, wo, keep, send, gain_part),
            [kept(F32, tokens, width), kept(BF16, tokens + extra, width)]
            + [flat] * 3 + [kept(F32, 1, width)],
            [pltpu.VMEM((tokens, inner), BF16)] * 4
            + [pltpu.VMEM((tokens, width), F32), pltpu.SemaphoreType.DMA((3,))],
            0, 0, 6 * unit_flops,
        )
        left.append(normed_t)
        context.append(ctx)
        grads_of.append((qg, kg, vg))
        cotangents.append(upstream)

        got = moves.flip(send, 1)
        own, to1, to2, to3, gain_sum = kernel_call(
            after_core, "after_core", (keep, got, gain_part),
            [kept(F32, 2 * rows, width)] + [kept(BF16, 2 * rows + extra, width)] * 3 + [kept(F32, 1, width)],
            [pltpu.VMEM((tokens, width), F32)],
        )
        got1, got2, got3 = moves.flip(to1, 4), moves.flip(to2, 8), moves.flip(to3, 12)
        if t == 0:
            read.append(recompute(1))
            beside = [read[1][5]]
        else:
            query_grad, key_grad = weight_grads(
                query_key_kernel, "query_key_grad", own, left,
                [grads_of[u][i] for i in range(2) for u in range(TICKS)], [], False,
            )
            value_grad, out_grad = weight_grads(
                value_out_kernel, "value_out_grad", own, left,
                [grads_of[u][2] for u in range(TICKS)] + context, cotangents, True,
            )
            beside = [from_hbm(query_grad), from_hbm(value_grad)]
        even, odd, gain_rows = kernel_call(
            after_column, "after_column",
            (own, z, block, gain, gain_sum, got1, got2, got3, *beside),
            [kept(BF16, rows, width)] * 2 + [kept(BF16, 16, width)], (), 0, len(beside),
        )
        even0, odd0 = moves.even(even, 0), moves.odd(odd, 0)
        even1, odd1 = moves.even(even, 2), moves.odd(odd, 2)
        (z,) = kernel_call(
            after_shift, "after_shift",
            (even0, even1, odd0, odd1, fresh[t]),
            [kept(BF16, 2 * rows, width)],
        )
        pieces = [z] + [moves.flip(z, 4 * j) for j in (1, 2, 3)]
        pieces = pieces + [moves.flip(p, 1) for p in pieces]
    last_inputs, last_cotangents, gain_grad = kernel_call(
        put_last, "put_last", (gain_rows, moves.flip(gain_rows, 2), *pieces),
        [shape(BF16, tokens, width)] * 2 + [shape(F32, 1, share)],
    )

    (shares,) = kernel_call(
        pick_share, "pick_share", (first_shares, current, to1), [kept(BF16, 2, share, tokens)],
        [pltpu.VMEM((width, tokens), BF16)], 0, 1,
    )
    (stored,) = kernel_call(
        put_store, "put_store", (reload_slot, store, moves.mirror(shares, 0)),
        [shape(BF16, *store.shape)], (), 1,
    )

    return (
        last_inputs[None],
        last_cotangents[None],
        jnp.swapaxes(stored, 1, 2)[None],
        query_grad[None],
        key_grad[None],
        value_grad[None],
        out_grad[None],
        gain_grad,
    )


def solution(mesh):
    placed = (
        P("section", None, None),
        P("section", None, None),
        P(),
        P(),
        P("section", None),
        P("section", None, "head"),
        P("section", None, "head"),
        P("section", None, "head"),
        P("section", "head", None),
        P("section", None, None, "head"),
        P(),
    )
    return jax.shard_map(
        per_device,
        mesh=mesh,
        in_specs=placed,
        out_specs=(
            P("section", None, None),
            P("section", None, None),
            P("section", None, None, "head"),
            P("section", None, "head"),
            P("section", None, "head"),
            P("section", None, "head"),
            P("section", "head", None),
            P("section", "head"),
        ),
        check_vma=False,
    )
```

```python
import jax
import jax.numpy as jnp
from jax import lax
from jax.experimental import pallas as pl
from jax.experimental.pallas import tpu as pltpu
from jax.sharding import PartitionSpec as P

DK = 128
TICKS = 2
SCALE = DK ** (-0.5)
EPSILON = 1e-06
BF16 = jnp.bfloat16
F32 = jnp.float32
NT = (((1,), (1,)), ((), ()))
TN = (((0,), (0,)), ((), ()))
MIB = 1024 * 1024


def dot(a, b):
    return jnp.dot(a, b, preferred_element_type=F32)


def dot_nt(a, b):
    return lax.dot_general(a, b, NT, preferred_element_type=F32)


def dot_tn(a, b):
    return lax.dot_general(a, b, TN, preferred_element_type=F32)


def normalize(rows, gain_row):
    floats = rows.astype(F32)
    inverse = lax.rsqrt(jnp.mean(floats * floats, axis=-1, keepdims=True) + EPSILON)
    unit_rows = floats * inverse
    return unit_rows * gain_row, unit_rows, inverse


def softmax(queries, key_rows):
    scores = dot_nt(queries, key_rows) * SCALE
    exponent = jnp.exp(scores - jnp.max(scores, axis=-1, keepdims=True))
    return exponent * (1.0 / jnp.sum(exponent, axis=-1, keepdims=True))


VMEM = pl.BlockSpec(memory_space=pltpu.VMEM)
SMEM = pl.BlockSpec(memory_space=pltpu.SMEM)
ANYWHERE = pl.BlockSpec(memory_space=pltpu.HBM)


def shape(dtype, *dims):
    return jax.ShapeDtypeStruct(dims, dtype)


def kept(dtype, *dims):
    return pltpu.VMEM(dims, dtype)


def in_hbm(dtype, *dims):
    return pltpu.HBM(dims, dtype)


def from_hbm(value):
    return pltpu.with_memory_space_constraint(value, pltpu.HBM)


def where_am_i():
    head = lax.axis_index("head")
    return head & 1, (head >> 1) & 1, head >> 2, lax.axis_index("section")


def kernel_call(body, name, args, outs, scratch=(), scalars=0, loose=0, flops=0, limit=16):
    moved = sum(a.size * a.dtype.itemsize for a in args)
    return pl.pallas_call(
        body,
        in_specs=[SMEM] * scalars + [VMEM] * (len(args) - scalars - loose) + [ANYWHERE] * loose,
        out_specs=[ANYWHERE if getattr(o, "memory_space", None) is pltpu.HBM else VMEM for o in outs],
        out_shape=list(outs),
        scratch_shapes=list(scratch),
        compiler_params=pltpu.CompilerParams(vmem_limit_bytes=limit * MIB),
        cost_estimate=pl.CostEstimate(flops=flops, bytes_accessed=moved, transcendentals=0),
        name=name,
    )(*args)


def lanes(i):
    return slice(i * DK, (i + 1) * DK)


def at_rows(start, count):
    return pl.ds(pl.multiple_of(start, count), count)


def run_copies(pairs, sems):
    copies = [pltpu.make_async_copy(src, dst, sems.at[i]) for i, (src, dst) in enumerate(pairs)]
    for copy in copies:
        copy.start()
    for copy in copies:
        copy.wait()


def pick_held(slots, store, out, sems):
    mirror = lax.axis_size("section") - 1 - lax.axis_index("section")
    run_copies([(store.at[slots[t, mirror]], out.at[t]) for t in range(TICKS)], sems)


def pick_rows(current, upstream, tokens, cotangents, z, *refs):
    *fresh, sems = refs
    core, _, column, _ = where_am_i()
    rows = z.shape[0] // 2
    at = at_rows(core * (current.shape[0] // 2) + column * rows, rows)
    pairs = [(current.at[at, :], z.at[:rows, :]), (upstream.at[at, :], z.at[rows:, :])]
    for t in range(TICKS):
        pairs.append((tokens.at[t, at, :], fresh[t].at[:rows, :]))
        pairs.append((cotangents.at[t, at, :], fresh[t].at[rows:, :]))
    run_copies(pairs, sems)


def turn_first(slots, current, gain, shares, flag, current_out, gain_out, turned):
    section, head = lax.axis_index("section"), lax.axis_index("head")
    share = shares.shape[1]
    turned[...] = current[...].T
    shares[0] = turned[at_rows(head * share, share), :]
    shares[1] = turned[at_rows((head ^ 2) * share, share), :]
    same = jnp.where(slots[0, section] == slots[1, section], 1.0, 0.0)
    flag[...] = jnp.full(flag.shape, same, F32)
    current_out[...] = current[...]
    gain_out[...] = gain[...]


def pick_reload(near, far, shares, flag, both):
    both[0] = near[0]
    both[1] = far[0]
    same = flag[0:1, :] > 0.5
    for y, ref in enumerate((near, far)):
        both[2 + y] = jnp.where(same, shares[y].astype(F32), ref[1].astype(F32)).astype(BF16)


def part_reload(own, got2, got1, got3, after, first, second):
    for j, ref in enumerate((own, got1, got2, got3)):
        first[2 * j : 2 * j + 2] = ref[0:2]
        second[2 * j : 2 * j + 2] = ref[2:4]


def pick_share(first_shares, current, after, out, turned):
    share = first_shares.shape[1]
    turned[...] = current[...].T
    out[0] = first_shares[0]
    out[1] = turned[at_rows(lax.axis_index("head") * share, share), :]


def attend_and_project(n, total, keep_ref, send_ref, wq, wk, wv, wo, q, k, v, context, ready):
    ready(0)
    q[...] = dot(n, wq[...]).astype(BF16)
    ready(1)
    k[...] = dot(n, wk[...]).astype(BF16)
    ready(2)
    v[...] = dot(n, wv[...]).astype(BF16)
    for i in range(q.shape[1] // DK):
        at = lanes(i)
        low = softmax(q[:, at], k[:, at]).astype(BF16)
        context[:, at] = dot(low, v[:, at]).astype(BF16)
    ready(3)
    total[...] = dot(context[...], wo[...])
    core = where_am_i()[0]
    half = keep_ref.shape[0]
    keep_ref[...] = total[at_rows(core * half, half), :]
    send_ref[...] = total[at_rows((1 - core) * half, half), :].astype(BF16)


def forward_first(rows, gain, hq, hk, hv, ho, wq, wk, wv, wo, keep, send, q, k, v, context, total, sems):
    copies = [
        pltpu.make_async_copy(src, dst, sems.at[i])
        for i, (src, dst) in enumerate(((hq, wq), (hk, wk), (hv, wv), (ho, wo)))
    ]
    for copy in copies:
        copy.start()
    n = normalize(rows[...], gain[...])[0].astype(BF16)
    attend_and_project(
        n, total, keep, send, wq, wk, wv, wo, q, k, v, context, lambda i: copies[i].wait()
    )


def put_pieces(pieces, first, second):
    core, _, column, _ = where_am_i()
    rows = pieces[0].shape[0] // 2
    half = first.shape[0] // 2
    for i, ref in enumerate(pieces):
        c = core if i < 4 else 1 - core
        at = at_rows(c * half + (column ^ (i % 4)) * rows, rows)
        first[at, :] = ref[:rows, :]
        second[at, :] = ref[rows:, :]


def forward_next(gain, wq, wk, wv, wo, *refs):
    pieces, (rows, g, keep, send), (q, k, v, context, total) = refs[:8], refs[8:12], refs[12:]
    put_pieces(pieces, rows, g)
    n = normalize(rows[...], gain[...])[0].astype(BF16)
    attend_and_project(n, total, keep, send, wq, wk, wv, wo, q, k, v, context, lambda i: None)


def put_last(slots, store, arrived, gain_rows, gain_other, *refs):
    pieces, (rows, g, stored, gain_out) = refs[:8], refs[8:]
    mirror = lax.axis_size("section") - 1 - lax.axis_index("section")
    stored[...] = store[...]
    for t in range(TICKS):
        stored[slots[t, mirror]] = arrived[t]
    put_pieces(pieces, rows, g)
    value = get_gain(gain_rows, 0) + get_gain(gain_other, 0)
    share = gain_out.shape[1]
    for h in range(value.shape[1] // share):

        @pl.when(lax.axis_index("head") == h)
        def _():
            gain_out[...] = value[:, h * share : (h + 1) * share]


def recompute_kernel(gain, wq, wk, wv, *refs):
    mine, other, block_ref, normed_t, q, k, v, soft, context, block_t = refs
    core, high, column, _ = where_am_i()
    share = mine.shape[1]
    for ref, c in ((mine, core), (other, 1 - core)):
        for i in range(8):
            head = (column ^ (i // 2)) * 4 + (high ^ (i % 2)) * 2 + c
            block_t[at_rows(head * share, share), :] = ref[i]
    block = block_t[...].T
    block_ref[...] = block
    n = normalize(block, gain[...])[0].astype(BF16)
    normed_t[...] = n.T
    q[...] = dot(n, wq[...]).astype(BF16)
    k[...] = dot(n, wk[...]).astype(BF16)
    v[...] = dot(n, wv[...]).astype(BF16)
    for i in range(q.shape[1] // DK):
        at = lanes(i)
        rows = softmax(q[:, at], k[:, at])
        soft[i] = rows
        context[:, at] = dot(rows.astype(BF16), v[:, at]).astype(BF16)


def backward_kernel(
    g, block, gain, q, k, v, soft, wq, wk, wv, wo, ahead_keep, ahead_send, gain_before,
    *refs,
):
    keep, send, qg, kg, vg, gain_part, grads, total = refs
    grads[...] = dot_nt(g[...], wo[...]).astype(BF16)
    for i in range(q.shape[1] // DK):
        at = lanes(i)
        rows = soft[i]
        grad = grads[:, at]
        soft_grad = dot_nt(grad, v[:, at])
        vg[:, at] = dot_tn(rows.astype(BF16), grad).astype(BF16)
        along = jnp.sum(rows * soft_grad, axis=-1, keepdims=True)
        score_grad = (rows * (soft_grad - along) * SCALE).astype(BF16)
        qg[:, at] = dot(score_grad, k[:, at]).astype(BF16)
        kg[:, at] = dot_tn(score_grad, q[:, at]).astype(BF16)
    total[...] = dot_nt(qg[...], wq[...])
    total[...] += dot_nt(kg[...], wk[...])
    total[...] += dot_nt(vg[...], wv[...])
    half = ahead_keep.shape[0]
    core = where_am_i()[0]
    keep[:half, :] = ahead_keep[...]
    keep[half:, :] = total[at_rows(core * half, half), :]
    send[:half, :] = ahead_send[...]
    send[half : 2 * half, :] = total[at_rows((1 - core) * half, half), :].astype(BF16)
    unit = normalize(block[...], gain[...])[1]
    part = gain_before[...] + jnp.sum(total[...] * unit, axis=0, keepdims=True)
    gain_part[...] = part
    if send.shape[0] > 2 * half:
        put_gain(send, 2 * half, part)


def put_gain(ref, row, value):
    value = jnp.broadcast_to(value, (16, value.shape[1]))
    high = value.astype(BF16)
    low = (value - high.astype(F32)).astype(BF16)
    is_first = lax.broadcasted_iota(jnp.int32, value.shape, 0) == 0
    ref[row : row + 16, :] = jnp.where(is_first, high.astype(F32), low.astype(F32)).astype(BF16)


def get_gain(ref, row):
    tile = ref[row : row + 16, :].astype(F32)
    return tile[0:1] + tile[1:2]


def after_core(keep, got, gain_part, *refs):
    own, to1, to2, to3, gain_out, mine = refs[-6:]
    column = where_am_i()[2]
    half = keep.shape[0] // 2
    rows = half // 4
    mine[...] = keep[...] + got[: 2 * half, :].astype(F32)
    for j, ref in ((0, own), (1, to1), (2, to2), (3, to3)):
        for part in range(2):
            at = at_rows(part * half + (column ^ j) * rows, rows)
            ref[part * rows : (part + 1) * rows, :] = mine[at, :].astype(ref.dtype)
    if got.shape[0] > 2 * half:
        value = gain_part[...] + get_gain(got, 2 * half)
        gain_out[...] = value
        for ref in (to1, to2, to3):
            put_gain(ref, 2 * rows, value)
    else:
        gain_out[...] = gain_part[...]


def after_column(own, z, block, gain, gain_part, got2, got1, got3, *refs):
    even, odd, gain_out = refs[-3:]
    core, high, column, section = where_am_i()
    rows = z.shape[0] // 2
    tokens = block.shape[0]
    total = [None, None]
    for part in range(2):
        at = slice(part * rows, (part + 1) * rows)
        total[part] = own[at, :] + (
            got1[at, :].astype(F32) + (got2[at, :].astype(F32) + got3[at, :].astype(F32))
        )
    here = jnp.where(high == 0, 1.0, 0.0).astype(F32)
    ahead = (here * z[:rows, :].astype(F32) + total[0]).astype(BF16)
    at = at_rows(core * (tokens // 2) + column * rows, rows)
    _, unit, inverse = normalize(block[at, :], gain[...])
    unit_grad = total[1] * gain[...]
    along = jnp.mean(unit_grad * unit, axis=-1, keepdims=True)
    back = here * z[rows:, :].astype(F32) + inverse * (unit_grad - unit * along)
    back = back.astype(BF16)

    @pl.when((section & 1) == 0)
    def _():
        even[...] = ahead
        odd[...] = back

    @pl.when((section & 1) == 1)
    def _():
        even[...] = back
        odd[...] = ahead

    if got1.shape[0] > 2 * rows:
        value = get_gain(got1, 2 * rows) + get_gain(got2, 2 * rows) + get_gain(got3, 2 * rows)
        put_gain(gain_out, 0, gain_part[...] + value)
    else:
        put_gain(gain_out, 0, gain_part[...])


def after_shift(even0, odd0, even1, odd1, fresh, *refs):
    z = refs[-1]
    section = where_am_i()[3]
    rows = even0.shape[0]
    even = (even0[...].astype(F32) + even1[...].astype(F32)).astype(BF16)
    odd = (odd0[...].astype(F32) + odd1[...].astype(F32)).astype(BF16)

    @pl.when((section & 1) == 0)
    def _():
        z[:rows, :] = odd
        z[rows:, :] = even

    @pl.when((section & 1) == 1)
    def _():
        z[:rows, :] = even
        z[rows:, :] = odd

    @pl.when(section == 0)
    def _():
        z[:rows, :] = fresh[:rows, :]

    @pl.when(section == lax.axis_size("section") - 1)
    def _():
        z[rows:, :] = fresh[rows:, :]


def step_lanes(ref):
    width = ref.shape[1] // pl.num_programs(0)
    return ref[:, pl.ds(pl.multiple_of(pl.program_id(0) * width, width), width)]


def weight_kernel(after, n0, n1, a0, a1, out):
    out[...] = (dot(n0[...], step_lanes(a0)) + dot(n1[...], step_lanes(a1))).astype(BF16)


def out_weight_kernel(after, c0, c1, g0, g1, out):
    out[...] = (dot_tn(step_lanes(c0), g0[...]) + dot_tn(step_lanes(c1), g1[...])).astype(BF16)


def weight_grad(name, after, left, right, by_rows=False):
    steps = 4
    tokens, cols = right[0].shape
    rows = left[0].shape[1] if by_rows else left[0].shape[0]
    if by_rows:
        out = pl.BlockSpec((rows // steps, cols), lambda i: (i, 0))
    else:
        out = pl.BlockSpec((rows, cols // steps), lambda i: (0, i))
    return pl.pallas_call(
        out_weight_kernel if by_rows else weight_kernel,
        grid=(steps,),
        in_specs=[pl.BlockSpec(memory_space=pl.ANY)] + [VMEM] * 4,
        out_specs=out,
        out_shape=shape(BF16, rows, cols),
        compiler_params=pltpu.CompilerParams(
            dimension_semantics=("arbitrary",), vmem_limit_bytes=16 * MIB
        ),
        cost_estimate=pl.CostEstimate(
            flops=4 * tokens * rows * cols, bytes_accessed=2 * rows * cols, transcendentals=0
        ),
        name=name,
    )(after, *left, *right)


class Moves:
    def __init__(self, sections, heads):
        self.sections, self.heads = sections, heads

    def send(self, value, to, mask):
        pairs = []
        for s in range(self.sections):
            t = to(s)
            if 0 <= t < self.sections:
                pairs += [(s * self.heads + h, t * self.heads + (h ^ mask)) for h in range(self.heads)]
        return lax.ppermute(value, ("section", "head"), pairs)

    def flip(self, value, mask):
        return self.send(value, lambda s: s, mask)

    def even(self, value, mask):
        return self.send(value, lambda s: s ^ 1, mask)

    def odd(self, value, mask):
        return self.send(value, lambda s: ((s - 1) ^ 1) + 1, mask)

    def mirror(self, value, mask):
        return self.send(value, lambda s: self.sections - 1 - s, mask)


def per_device(
    section_inputs, section_cotangents, fresh_tokens, fresh_cotangents, norm_gain,
    query_weight, key_weight, value_weight, out_weight, saved_inputs, reload_slot,
):
    sections, heads = lax.axis_size("section"), lax.axis_size("head")
    section, head = lax.axis_index("section"), lax.axis_index("head")
    moves = Moves(sections, heads)
    share = saved_inputs.shape[3]
    gain = norm_gain
    store = jnp.swapaxes(saved_inputs[0], 1, 2)
    tokens, width = section_inputs.shape[1:]
    inner = query_weight.shape[2]
    half, rows = tokens // 2, tokens // 8
    unit_flops = 2 * tokens * width * inner
    current, upstream = section_inputs[0], section_cotangents[0]

    (going,) = kernel_call(
        pick_held, "pick_held", (reload_slot, from_hbm(store)), [kept(BF16, TICKS, share, tokens)],
        [pltpu.SemaphoreType.DMA((TICKS,))], 1, 1,
    )
    near, far = moves.mirror(going, 0), moves.mirror(going, 2)
    z, *fresh = kernel_call(
        pick_rows, "pick_rows",
        [from_hbm(a) for a in (current, upstream, fresh_tokens, fresh_cotangents)],
        [kept(BF16, 2 * rows, width)] * (1 + TICKS),
        [pltpu.SemaphoreType.DMA((2 + 2 * TICKS,))], 0, 4,
    )
    first_shares, flag, first_inputs, gain = kernel_call(
        turn_first, "turn_first", (reload_slot, current, gain),
        [
            kept(BF16, 2, share, tokens), kept(F32, 8, tokens),
            kept(BF16, tokens, width), kept(F32, 1, width),
        ],
        [pltpu.VMEM((width, tokens), BF16)], 1,
    )
    (both,) = kernel_call(
        pick_reload, "pick_reload", (near, far, first_shares, flag),
        [kept(BF16, 2 * TICKS, share, tokens)],
    )
    far_shares = moves.flip(both, 8)
    arriving = [both, far_shares, moves.flip(both, 4), moves.flip(both, 12)]

    flat = kept(BF16, tokens, inner)
    whole = kept(BF16, tokens, width)
    half_outs = [kept(F32, half, width), kept(BF16, half, width)]
    work = [pltpu.VMEM((tokens, inner), BF16)] * 4 + [pltpu.VMEM((tokens, width), F32)]
    gain_part = jnp.zeros((1, width), F32)
    left, context, grads_of, cotangents = [], [], [], []
    pieces = None

    def recompute(u):
        return kernel_call(
            recompute_kernel, "recompute", (gain, wq, wk, wv, *reload[u]),
            [
                whole, kept(BF16, width, tokens), flat, flat, flat,
                kept(F32, inner // DK, tokens, tokens), flat,
            ],
            [pltpu.VMEM((width, tokens), BF16)], 0, 0, 5 * unit_flops,
        )

    for t in range(TICKS):
        if t == 0:
            raw = [
                from_hbm(w[0]) for w in (query_weight, key_weight, value_weight, out_weight)
            ]
            *weights, keep, send = kernel_call(
                forward_first, "forward_first", (first_inputs, gain, *raw),
                [kept(BF16, *w.shape) for w in raw] + half_outs,
                work + [pltpu.SemaphoreType.DMA((4,))], 0, 4, 5 * unit_flops,
            )
            wq, wk, wv, wo = weights
            own_shares = kernel_call(
                part_reload, "part_reload", (*arriving, send),
                [kept(BF16, 8, share, tokens)] * TICKS, (), 0, 1,
            )
            reload = [(a, moves.flip(a, 1)) for a in own_shares]
        else:
            current, upstream, keep, send = kernel_call(
                forward_next, "forward_next", (gain, wq, wk, wv, wo, *pieces),
                [whole] * 2 + half_outs, work, 0, 0, 5 * unit_flops,
            )
        if t == 0:
            read = [recompute(u) for u in range(1)]
        block, normed_t, q, k, v, soft, ctx = read[t]
        extra = 16 if t == TICKS - 1 else 0
        keep, send, qg, kg, vg, gain_part = kernel_call(
            backward_kernel, "backward",
            (upstream, block, gain, q, k, v, soft, wq, wk, wv, wo, keep, send, gain_part),
            [kept(F32, tokens, width), kept(BF16, tokens + extra, width)]
            + [flat] * 3 + [kept(F32, 1, width)],
            [pltpu.VMEM((tokens, inner), BF16), pltpu.VMEM((tokens, width), F32)],
            0, 0, 6 * unit_flops,
        )
        left.append(normed_t)
        context.append(ctx)
        grads_of.append((qg, kg, vg))
        cotangents.append(upstream)

        got = moves.flip(send, 1)
        last = t == TICKS - 1
        if last:
            grads_of = [[grads_of[u][i] for u in range(TICKS)] for i in range(3)]
            query_grad = weight_grad("query_grad", gain_part, left, grads_of[0])
        beside = [from_hbm(query_grad)] if last else []
        own, to1, to2, to3, gain_sum = kernel_call(
            after_core, "after_core", (keep, got, gain_part, *beside),
            [kept(F32, 2 * rows, width)] + [kept(BF16, 2 * rows + extra, width)] * 3 + [kept(F32, 1, width)],
            [pltpu.VMEM((tokens, width), F32)], 0, len(beside),
        )
        got2 = moves.flip(to2, 8)
        got1, got3 = moves.flip(to1, 4), moves.flip(to3, 12)
        if last:
            key_grad = weight_grad("key_grad", own, left, grads_of[1])
            value_grad = weight_grad("value_grad", own, left, grads_of[2])
            (shares,) = kernel_call(
                pick_share, "pick_share", (first_shares, current, from_hbm(key_grad)), [kept(BF16, 2, share, tokens)],
                [pltpu.VMEM((width, tokens), BF16)], 0, 1,
            )
            arrived = moves.mirror(shares, 0)
            beside = [from_hbm(key_grad), from_hbm(value_grad), arrived]
        else:
            read.append(recompute(1))
            beside = [read[1][5]]
        even, odd, gain_rows = kernel_call(
            after_column, "after_column",
            (own, z, block, gain, gain_sum, got2, got1, got3, *beside),
            [kept(BF16, rows, width)] * 2 + [kept(BF16, 16, width)], (), 0, len(beside),
        )
        even0, odd0 = moves.even(even, 0), moves.odd(odd, 0)
        even1, odd1 = moves.even(even, 2), moves.odd(odd, 2)
        if last:
            out_grad = weight_grad("out_grad", even, context, cotangents, True)
            gain_other = moves.flip(gain_rows, 2)
            beside = [gain_other, from_hbm(out_grad)]
        else:
            beside = []
        (z,) = kernel_call(
            after_shift, "after_shift", (even0, odd0, even1, odd1, fresh[t], *beside),
            [kept(BF16, 2 * rows, width)], (), 0, len(beside),
        )
        pieces = [z] + [moves.flip(z, 4 * j) for j in (1, 2, 3)]
        pieces = pieces + [moves.flip(p, 1) for p in pieces]
    last_inputs, last_cotangents, stored, gain_grad = kernel_call(
        put_last, "put_last", (reload_slot, store, arrived, gain_rows, gain_other, *pieces),
        [shape(BF16, tokens, width)] * 2 + [shape(BF16, *store.shape), shape(F32, 1, share)], (), 1,
    )
    return (
        last_inputs[None],
        last_cotangents[None],
        jnp.swapaxes(stored, 1, 2)[None],
        query_grad[None],
        key_grad[None],
        value_grad[None],
        out_grad[None],
        gain_grad,
    )


def solution(mesh):
    placed = (
        P("section", None, None),
        P("section", None, None),
        P(),
        P(),
        P("section", None),
        P("section", None, "head"),
        P("section", None, "head"),
        P("section", None, "head"),
        P("section", "head", None),
        P("section", None, None, "head"),
        P(),
    )
    return jax.shard_map(
        per_device,
        mesh=mesh,
        in_specs=placed,
        out_specs=(
            P("section", None, None),
            P("section", None, None),
            P("section", None, None, "head"),
            P("section", None, "head"),
            P("section", None, "head"),
            P("section", None, "head"),
            P("section", "head", None),
            P("section", "head"),
        ),
        check_vma=False,
    )
```

```python
import jax
import jax.numpy as jnp
from jax import lax
from jax.experimental import pallas as pl
from jax.experimental.pallas import tpu as pltpu
from jax.sharding import PartitionSpec as P

DK = 128
TICKS = 2
SCALE = DK ** (-0.5)
EPSILON = 1e-06
BF16 = jnp.bfloat16
F32 = jnp.float32
NT = (((1,), (1,)), ((), ()))
TN = (((0,), (0,)), ((), ()))
MIB = 1024 * 1024


def dot(a, b):
    return jnp.dot(a, b, preferred_element_type=F32)


def dot_nt(a, b):
    return lax.dot_general(a, b, NT, preferred_element_type=F32)


def dot_tn(a, b):
    return lax.dot_general(a, b, TN, preferred_element_type=F32)


def normalize(rows, gain_row):
    floats = rows.astype(F32)
    inverse = lax.rsqrt(jnp.mean(floats * floats, axis=-1, keepdims=True) + EPSILON)
    unit_rows = floats * inverse
    return unit_rows * gain_row, unit_rows, inverse


def softmax(queries, key_rows):
    scores = dot_nt(queries, key_rows) * SCALE
    exponent = jnp.exp(scores - jnp.max(scores, axis=-1, keepdims=True))
    return exponent * (1.0 / jnp.sum(exponent, axis=-1, keepdims=True))


VMEM = pl.BlockSpec(memory_space=pltpu.VMEM)
SMEM = pl.BlockSpec(memory_space=pltpu.SMEM)
ANYWHERE = pl.BlockSpec(memory_space=pltpu.HBM)


def shape(dtype, *dims):
    return jax.ShapeDtypeStruct(dims, dtype)


def kept(dtype, *dims):
    return pltpu.VMEM(dims, dtype)


def in_hbm(dtype, *dims):
    return pltpu.HBM(dims, dtype)


def from_hbm(value):
    return pltpu.with_memory_space_constraint(value, pltpu.HBM)


def where_am_i():
    head = lax.axis_index("head")
    return head & 1, (head >> 1) & 1, head >> 2, lax.axis_index("section")


def kernel_call(body, name, args, outs, scratch=(), scalars=0, loose=0, flops=0, limit=16):
    moved = sum(a.size * a.dtype.itemsize for a in args)
    return pl.pallas_call(
        body,
        in_specs=[SMEM] * scalars + [VMEM] * (len(args) - scalars - loose) + [ANYWHERE] * loose,
        out_specs=[ANYWHERE if getattr(o, "memory_space", None) is pltpu.HBM else VMEM for o in outs],
        out_shape=list(outs),
        scratch_shapes=list(scratch),
        compiler_params=pltpu.CompilerParams(vmem_limit_bytes=limit * MIB),
        cost_estimate=pl.CostEstimate(flops=flops, bytes_accessed=moved, transcendentals=0),
        name=name,
    )(*args)


def lanes(i):
    return slice(i * DK, (i + 1) * DK)


def at_rows(start, count):
    return pl.ds(pl.multiple_of(start, count), count)


def run_copies(pairs, sems):
    copies = [pltpu.make_async_copy(src, dst, sems.at[i]) for i, (src, dst) in enumerate(pairs)]
    for copy in copies:
        copy.start()
    for copy in copies:
        copy.wait()


def pick_held(slots, store, out, sems):
    mirror = lax.axis_size("section") - 1 - lax.axis_index("section")
    run_copies([(store.at[slots[t, mirror]], out.at[t]) for t in range(TICKS)], sems)


def pick_rows(current, upstream, tokens, cotangents, z, *refs):
    *fresh, sems = refs
    core, _, column, _ = where_am_i()
    rows = z.shape[0] // 2
    at = at_rows(core * (current.shape[0] // 2) + column * rows, rows)
    pairs = [(current.at[at, :], z.at[:rows, :]), (upstream.at[at, :], z.at[rows:, :])]
    for t in range(TICKS):
        pairs.append((tokens.at[t, at, :], fresh[t].at[:rows, :]))
        pairs.append((cotangents.at[t, at, :], fresh[t].at[rows:, :]))
    run_copies(pairs, sems)


def turn_first(slots, current, gain, shares, flag, current_out, gain_out, turned):
    section, head = lax.axis_index("section"), lax.axis_index("head")
    share = shares.shape[1]
    turned[...] = current[...].T
    shares[0] = turned[at_rows(head * share, share), :]
    shares[1] = turned[at_rows((head ^ 2) * share, share), :]
    same = jnp.where(slots[0, section] == slots[1, section], 1.0, 0.0)
    flag[...] = jnp.full(flag.shape, same, F32)
    current_out[...] = current[...]
    gain_out[...] = gain[...]


def pick_reload(near, far, shares, flag, both):
    both[0] = near[0]
    both[1] = far[0]
    same = flag[0:1, :] > 0.5
    for y, ref in enumerate((near, far)):
        both[2 + y] = jnp.where(same, shares[y].astype(F32), ref[1].astype(F32)).astype(BF16)


def part_reload(own, got2, got1, got3, after, first, second):
    for j, ref in enumerate((own, got1, got2, got3)):
        first[2 * j : 2 * j + 2] = ref[0:2]
        second[2 * j : 2 * j + 2] = ref[2:4]


def pick_share(first_shares, current, out, turned):
    share = first_shares.shape[1]
    turned[...] = current[...].T
    out[0] = first_shares[0]
    out[1] = turned[at_rows(lax.axis_index("head") * share, share), :]


def attend_and_project(n, total, keep_ref, send_ref, wq, wk, wv, wo, q, k, v, context, ready):
    ready(0)
    q[...] = dot(n, wq[...]).astype(BF16)
    ready(1)
    k[...] = dot(n, wk[...]).astype(BF16)
    ready(2)
    v[...] = dot(n, wv[...]).astype(BF16)
    for i in range(q.shape[1] // DK):
        at = lanes(i)
        low = softmax(q[:, at], k[:, at]).astype(BF16)
        context[:, at] = dot(low, v[:, at]).astype(BF16)
    ready(3)
    total[...] = dot(context[...], wo[...])
    core = where_am_i()[0]
    half = keep_ref.shape[0]
    keep_ref[...] = total[at_rows(core * half, half), :]
    send_ref[...] = total[at_rows((1 - core) * half, half), :].astype(BF16)


def forward_first(rows, gain, hq, hk, hv, ho, wq, wk, wv, wo, keep, send, q, k, v, context, total, sems):
    copies = [
        pltpu.make_async_copy(src, dst, sems.at[i])
        for i, (src, dst) in enumerate(((hq, wq), (hk, wk), (hv, wv), (ho, wo)))
    ]
    for copy in copies:
        copy.start()
    n = normalize(rows[...], gain[...])[0].astype(BF16)
    attend_and_project(
        n, total, keep, send, wq, wk, wv, wo, q, k, v, context, lambda i: copies[i].wait()
    )


def put_pieces(pieces, first, second):
    core, _, column, _ = where_am_i()
    rows = pieces[0].shape[0] // 2
    half = first.shape[0] // 2
    for i, ref in enumerate(pieces):
        c = core if i < 4 else 1 - core
        at = at_rows(c * half + (column ^ (i % 4)) * rows, rows)
        first[at, :] = ref[:rows, :]
        second[at, :] = ref[rows:, :]


def forward_next(gain, wq, wk, wv, wo, *refs):
    pieces, (rows, g, keep, send), (q, k, v, context, total) = refs[:8], refs[8:12], refs[12:]
    put_pieces(pieces, rows, g)
    n = normalize(rows[...], gain[...])[0].astype(BF16)
    attend_and_project(n, total, keep, send, wq, wk, wv, wo, q, k, v, context, lambda i: None)


def put_last(slots, store, arrived, gain_rows, gain_other, *refs):
    pieces, (rows, g, stored, gain_out) = refs[:8], refs[8:]
    mirror = lax.axis_size("section") - 1 - lax.axis_index("section")
    stored[...] = store[...]
    for t in range(TICKS):
        stored[slots[t, mirror]] = arrived[t]
    put_pieces(pieces, rows, g)
    value = get_gain(gain_rows, 0) + get_gain(gain_other, 0)
    share = gain_out.shape[1]
    for h in range(value.shape[1] // share):

        @pl.when(lax.axis_index("head") == h)
        def _():
            gain_out[...] = value[:, h * share : (h + 1) * share]


def recompute_kernel(gain, wq, wk, wv, *refs):
    mine, other, block_ref, normed_t, q, k, v, soft, context, block_t = refs
    core, high, column, _ = where_am_i()
    share = mine.shape[1]
    for ref, c in ((mine, core), (other, 1 - core)):
        for i in range(8):
            head = (column ^ (i // 2)) * 4 + (high ^ (i % 2)) * 2 + c
            block_t[at_rows(head * share, share), :] = ref[i]
    block = block_t[...].T
    block_ref[...] = block
    n = normalize(block, gain[...])[0].astype(BF16)
    normed_t[...] = n.T
    q[...] = dot(n, wq[...]).astype(BF16)
    k[...] = dot(n, wk[...]).astype(BF16)
    v[...] = dot(n, wv[...]).astype(BF16)
    for i in range(q.shape[1] // DK):
        at = lanes(i)
        rows = softmax(q[:, at], k[:, at])
        soft[i] = rows
        context[:, at] = dot(rows.astype(BF16), v[:, at]).astype(BF16)


def backward_kernel(
    g, block, gain, q, k, v, soft, wq, wk, wv, wo, ahead_keep, ahead_send, gain_before,
    *refs,
):
    keep, send, qg, kg, vg, gain_part, grads, total = refs
    grads[...] = dot_nt(g[...], wo[...]).astype(BF16)
    for i in range(q.shape[1] // DK):
        at = lanes(i)
        rows = soft[i]
        grad = grads[:, at]
        soft_grad = dot_nt(grad, v[:, at])
        vg[:, at] = dot_tn(rows.astype(BF16), grad).astype(BF16)
        along = jnp.sum(rows * soft_grad, axis=-1, keepdims=True)
        score_grad = (rows * (soft_grad - along) * SCALE).astype(BF16)
        qg[:, at] = dot(score_grad, k[:, at]).astype(BF16)
        kg[:, at] = dot_tn(score_grad, q[:, at]).astype(BF16)
    total[...] = dot_nt(qg[...], wq[...])
    total[...] += dot_nt(kg[...], wk[...])
    total[...] += dot_nt(vg[...], wv[...])
    half = ahead_keep.shape[0]
    core = where_am_i()[0]
    keep[:half, :] = ahead_keep[...]
    keep[half:, :] = total[at_rows(core * half, half), :]
    send[:half, :] = ahead_send[...]
    send[half : 2 * half, :] = total[at_rows((1 - core) * half, half), :].astype(BF16)
    unit = normalize(block[...], gain[...])[1]
    part = gain_before[...] + jnp.sum(total[...] * unit, axis=0, keepdims=True)
    gain_part[...] = part
    if send.shape[0] > 2 * half:
        put_gain(send, 2 * half, part)


def put_gain(ref, row, value):
    value = jnp.broadcast_to(value, (16, value.shape[1]))
    high = value.astype(BF16)
    low = (value - high.astype(F32)).astype(BF16)
    is_first = lax.broadcasted_iota(jnp.int32, value.shape, 0) == 0
    ref[row : row + 16, :] = jnp.where(is_first, high.astype(F32), low.astype(F32)).astype(BF16)


def get_gain(ref, row):
    tile = ref[row : row + 16, :].astype(F32)
    return tile[0:1] + tile[1:2]


def after_core(keep, got, gain_part, *refs):
    own, to1, to2, to3, gain_out, mine = refs[-6:]
    column = where_am_i()[2]
    half = keep.shape[0] // 2
    rows = half // 4
    mine[...] = keep[...] + got[: 2 * half, :].astype(F32)
    for j, ref in ((0, own), (1, to1), (2, to2), (3, to3)):
        for part in range(2):
            at = at_rows(part * half + (column ^ j) * rows, rows)
            ref[part * rows : (part + 1) * rows, :] = mine[at, :].astype(ref.dtype)
    if got.shape[0] > 2 * half:
        value = gain_part[...] + get_gain(got, 2 * half)
        gain_out[...] = value
        for ref in (to1, to2, to3):
            put_gain(ref, 2 * rows, value)
    else:
        gain_out[...] = gain_part[...]


def after_column(own, z, block, gain, gain_part, got2, got1, got3, *refs):
    even, odd, gain_out = refs[-3:]
    core, high, column, section = where_am_i()
    rows = z.shape[0] // 2
    tokens = block.shape[0]
    total = [None, None]
    for part in range(2):
        at = slice(part * rows, (part + 1) * rows)
        total[part] = own[at, :] + (
            got1[at, :].astype(F32) + (got2[at, :].astype(F32) + got3[at, :].astype(F32))
        )
    here = jnp.where(high == 0, 1.0, 0.0).astype(F32)
    ahead = (here * z[:rows, :].astype(F32) + total[0]).astype(BF16)
    at = at_rows(core * (tokens // 2) + column * rows, rows)
    _, unit, inverse = normalize(block[at, :], gain[...])
    unit_grad = total[1] * gain[...]
    along = jnp.mean(unit_grad * unit, axis=-1, keepdims=True)
    back = here * z[rows:, :].astype(F32) + inverse * (unit_grad - unit * along)
    back = back.astype(BF16)

    @pl.when((section & 1) == 0)
    def _():
        even[...] = ahead
        odd[...] = back

    @pl.when((section & 1) == 1)
    def _():
        even[...] = back
        odd[...] = ahead

    if got1.shape[0] > 2 * rows:
        value = get_gain(got1, 2 * rows) + get_gain(got2, 2 * rows) + get_gain(got3, 2 * rows)
        put_gain(gain_out, 0, gain_part[...] + value)
    else:
        put_gain(gain_out, 0, gain_part[...])


def after_shift(even0, odd0, even1, odd1, fresh, *refs):
    z = refs[-1]
    section = where_am_i()[3]
    rows = even0.shape[0]
    even = (even0[...].astype(F32) + even1[...].astype(F32)).astype(BF16)
    odd = (odd0[...].astype(F32) + odd1[...].astype(F32)).astype(BF16)

    @pl.when((section & 1) == 0)
    def _():
        z[:rows, :] = odd
        z[rows:, :] = even

    @pl.when((section & 1) == 1)
    def _():
        z[:rows, :] = even
        z[rows:, :] = odd

    @pl.when(section == 0)
    def _():
        z[:rows, :] = fresh[:rows, :]

    @pl.when(section == lax.axis_size("section") - 1)
    def _():
        z[rows:, :] = fresh[rows:, :]


def step_block(ref, axis):
    size = ref.shape[axis] // pl.num_programs(0)
    at = pl.ds(pl.multiple_of(pl.program_id(0) * size, size), size)
    return ref[at, :] if axis == 0 else ref[:, at]


def in_weight_kernel(after, n0, n1, *refs):
    left, right = step_block(n0, 0), step_block(n1, 0)
    for i in range(3):
        refs[6 + i][...] = (dot(left, refs[2 * i][...]) + dot(right, refs[2 * i + 1][...])).astype(BF16)


def out_weight_kernel(after, c0, c1, g0, g1, out):
    out[...] = (dot_tn(step_block(c0, 1), g0[...]) + dot_tn(step_block(c1, 1), g1[...])).astype(BF16)


def weight_grads(body, name, after, args, rows, count):
    steps = 4
    tokens, cols = args[-1].shape
    return pl.pallas_call(
        body,
        grid=(steps,),
        in_specs=[pl.BlockSpec(memory_space=pl.ANY)] + [VMEM] * len(args),
        out_specs=[pl.BlockSpec((rows // steps, cols), lambda i: (i, 0))] * count,
        out_shape=[shape(BF16, rows, cols)] * count,
        compiler_params=pltpu.CompilerParams(
            dimension_semantics=("arbitrary",), vmem_limit_bytes=16 * MIB
        ),
        cost_estimate=pl.CostEstimate(
            flops=4 * count * tokens * rows * cols, bytes_accessed=2 * count * rows * cols, transcendentals=0
        ),
        name=name,
    )(after, *args)


class Moves:
    def __init__(self, sections, heads):
        self.sections, self.heads = sections, heads

    def send(self, value, to, mask):
        pairs = []
        for s in range(self.sections):
            t = to(s)
            if 0 <= t < self.sections:
                pairs += [(s * self.heads + h, t * self.heads + (h ^ mask)) for h in range(self.heads)]
        return lax.ppermute(value, ("section", "head"), pairs)

    def flip(self, value, mask):
        return self.send(value, lambda s: s, mask)

    def even(self, value, mask):
        return self.send(value, lambda s: s ^ 1, mask)

    def odd(self, value, mask):
        return self.send(value, lambda s: ((s - 1) ^ 1) + 1, mask)

    def mirror(self, value, mask):
        return self.send(value, lambda s: self.sections - 1 - s, mask)


def per_device(
    section_inputs, section_cotangents, fresh_tokens, fresh_cotangents, norm_gain,
    query_weight, key_weight, value_weight, out_weight, saved_inputs, reload_slot,
):
    sections, heads = lax.axis_size("section"), lax.axis_size("head")
    section, head = lax.axis_index("section"), lax.axis_index("head")
    moves = Moves(sections, heads)
    share = saved_inputs.shape[3]
    gain = norm_gain
    store = jnp.swapaxes(saved_inputs[0], 1, 2)
    tokens, width = section_inputs.shape[1:]
    inner = query_weight.shape[2]
    half, rows = tokens // 2, tokens // 8
    unit_flops = 2 * tokens * width * inner
    current, upstream = section_inputs[0], section_cotangents[0]

    (going,) = kernel_call(
        pick_held, "pick_held", (reload_slot, from_hbm(store)), [kept(BF16, TICKS, share, tokens)],
        [pltpu.SemaphoreType.DMA((TICKS,))], 1, 1,
    )
    near, far = moves.mirror(going, 0), moves.mirror(going, 2)
    z, *fresh = kernel_call(
        pick_rows, "pick_rows",
        [from_hbm(a) for a in (current, upstream, fresh_tokens, fresh_cotangents)],
        [kept(BF16, 2 * rows, width)] * (1 + TICKS),
        [pltpu.SemaphoreType.DMA((2 + 2 * TICKS,))], 0, 4,
    )
    first_shares, flag, first_inputs, gain = kernel_call(
        turn_first, "turn_first", (reload_slot, current, gain),
        [
            kept(BF16, 2, share, tokens), kept(F32, 8, tokens),
            kept(BF16, tokens, width), kept(F32, 1, width),
        ],
        [pltpu.VMEM((width, tokens), BF16)], 1,
    )
    (both,) = kernel_call(
        pick_reload, "pick_reload", (near, far, first_shares, flag),
        [kept(BF16, 2 * TICKS, share, tokens)],
    )
    far_shares = moves.flip(both, 8)
    arriving = [both, far_shares, moves.flip(both, 4), moves.flip(both, 12)]

    flat = kept(BF16, tokens, inner)
    whole = kept(BF16, tokens, width)
    half_outs = [kept(F32, half, width), kept(BF16, half, width)]
    work = [pltpu.VMEM((tokens, inner), BF16)] * 4 + [pltpu.VMEM((tokens, width), F32)]
    gain_part = jnp.zeros((1, width), F32)
    left, context, grads_of, cotangents = [], [], [], []
    pieces = None

    def recompute(u):
        return kernel_call(
            recompute_kernel, "recompute", (gain, wq, wk, wv, *reload[u]),
            [
                whole, kept(BF16, width, tokens), flat, flat, flat,
                kept(F32, inner // DK, tokens, tokens), flat,
            ],
            [pltpu.VMEM((width, tokens), BF16)], 0, 0, 5 * unit_flops,
        )

    for t in range(TICKS):
        if t == 0:
            raw = [
                from_hbm(w[0]) for w in (query_weight, key_weight, value_weight, out_weight)
            ]
            *weights, keep, send = kernel_call(
                forward_first, "forward_first", (first_inputs, gain, *raw),
                [kept(BF16, *w.shape) for w in raw] + half_outs,
                work + [pltpu.SemaphoreType.DMA((4,))], 0, 4, 5 * unit_flops,
            )
            wq, wk, wv, wo = weights
            own_shares = kernel_call(
                part_reload, "part_reload", (*arriving, send),
                [kept(BF16, 8, share, tokens)] * TICKS, (), 0, 1,
            )
            reload = [(a, moves.flip(a, 1)) for a in own_shares]
        else:
            current, upstream, keep, send = kernel_call(
                forward_next, "forward_next", (gain, wq, wk, wv, wo, *pieces),
                [whole] * 2 + half_outs, work, 0, 0, 5 * unit_flops,
            )
        if t == 0:
            read = [recompute(u) for u in range(1)]
        block, normed_t, q, k, v, soft, ctx = read[t]
        extra = 16 if t == TICKS - 1 else 0
        keep, send, qg, kg, vg, gain_part = kernel_call(
            backward_kernel, "backward",
            (upstream, block, gain, q, k, v, soft, wq, wk, wv, wo, keep, send, gain_part),
            [kept(F32, tokens, width), kept(BF16, tokens + extra, width)]
            + [flat] * 3 + [kept(F32, 1, width)],
            [pltpu.VMEM((tokens, inner), BF16), pltpu.VMEM((tokens, width), F32)],
            0, 0, 6 * unit_flops,
        )
        left.append(normed_t)
        context.append(ctx)
        grads_of.append((qg, kg, vg))
        cotangents.append(upstream)

        got = moves.flip(send, 1)
        last = t == TICKS - 1
        if last:
            (shares,) = kernel_call(
                pick_share, "pick_share", (first_shares, current), [kept(BF16, 2, share, tokens)],
                [pltpu.VMEM((width, tokens), BF16)],
            )
            arrived = moves.mirror(shares, 0)
        beside = [shares] if last else []
        own, to1, to2, to3, gain_sum = kernel_call(
            after_core, "after_core", (keep, got, gain_part, *beside),
            [kept(F32, 2 * rows, width)] + [kept(BF16, 2 * rows + extra, width)] * 3 + [kept(F32, 1, width)],
            [pltpu.VMEM((tokens, width), F32)], 0, len(beside),
        )
        got2 = moves.flip(to2, 8)
        got1, got3 = moves.flip(to1, 4), moves.flip(to3, 12)
        if last:
            query_grad, key_grad, value_grad = weight_grads(
                in_weight_kernel, "in_grads", own,
                [*left, *[grads_of[u][i] for i in range(3) for u in range(TICKS)]], width, 3,
            )
            beside = [from_hbm(query_grad), arrived]
        else:
            read.append(recompute(1))
            beside = [read[1][5]]
        even, odd, gain_rows = kernel_call(
            after_column, "after_column",
            (own, z, block, gain, gain_sum, got2, got1, got3, *beside),
            [kept(BF16, rows, width)] * 2 + [kept(BF16, 16, width)], (), 0, len(beside),
        )
        even0, odd0 = moves.even(even, 0), moves.odd(odd, 0)
        even1, odd1 = moves.even(even, 2), moves.odd(odd, 2)
        if last:
            (out_grad,) = weight_grads(
                out_weight_kernel, "out_grad", even, [*context, *cotangents], inner, 1
            )
            gain_other = moves.flip(gain_rows, 2)
            beside = [gain_other, from_hbm(out_grad)]
        else:
            beside = []
        (z,) = kernel_call(
            after_shift, "after_shift", (even0, odd0, even1, odd1, fresh[t], *beside),
            [kept(BF16, 2 * rows, width)], (), 0, len(beside),
        )
        pieces = [z] + [moves.flip(z, 4 * j) for j in (1, 2, 3)]
        pieces = pieces + [moves.flip(p, 1) for p in pieces]
    last_inputs, last_cotangents, stored, gain_grad = kernel_call(
        put_last, "put_last", (reload_slot, store, arrived, gain_rows, gain_other, *pieces),
        [shape(BF16, tokens, width)] * 2 + [shape(BF16, *store.shape), shape(F32, 1, share)], (), 1,
    )
    return (
        last_inputs[None],
        last_cotangents[None],
        jnp.swapaxes(stored, 1, 2)[None],
        query_grad[None],
        key_grad[None],
        value_grad[None],
        out_grad[None],
        gain_grad,
    )


def solution(mesh):
    placed = (
        P("section", None, None),
        P("section", None, None),
        P(),
        P(),
        P("section", None),
        P("section", None, "head"),
        P("section", None, "head"),
        P("section", None, "head"),
        P("section", "head", None),
        P("section", None, None, "head"),
        P(),
    )
    return jax.shard_map(
        per_device,
        mesh=mesh,
        in_specs=placed,
        out_specs=(
            P("section", None, None),
            P("section", None, None),
            P("section", None, None, "head"),
            P("section", None, "head"),
            P("section", None, "head"),
            P("section", None, "head"),
            P("section", "head", None),
            P("section", "head"),
        ),
        check_vma=False,
    )
```

```python
import jax
import jax.numpy as jnp
from jax import lax
from jax.experimental import pallas as pl
from jax.experimental.pallas import tpu as pltpu
from jax.sharding import PartitionSpec as P

DK = 128
TICKS = 2
SCALE = DK ** (-0.5)
EPSILON = 1e-06
BF16 = jnp.bfloat16
F32 = jnp.float32
NT = (((1,), (1,)), ((), ()))
TN = (((0,), (0,)), ((), ()))
MIB = 1024 * 1024


def dot(a, b):
    return jnp.dot(a, b, preferred_element_type=F32)


def dot_nt(a, b):
    return lax.dot_general(a, b, NT, preferred_element_type=F32)


def dot_tn(a, b):
    return lax.dot_general(a, b, TN, preferred_element_type=F32)


def normalize(rows, gain_row):
    floats = rows.astype(F32)
    inverse = lax.rsqrt(jnp.mean(floats * floats, axis=-1, keepdims=True) + EPSILON)
    unit_rows = floats * inverse
    return unit_rows * gain_row, unit_rows, inverse


def softmax(queries, key_rows):
    scores = dot_nt(queries, key_rows) * SCALE
    exponent = jnp.exp(scores - jnp.max(scores, axis=-1, keepdims=True))
    return exponent * (1.0 / jnp.sum(exponent, axis=-1, keepdims=True))


VMEM = pl.BlockSpec(memory_space=pltpu.VMEM)
SMEM = pl.BlockSpec(memory_space=pltpu.SMEM)
ANYWHERE = pl.BlockSpec(memory_space=pltpu.HBM)


def shape(dtype, *dims):
    return jax.ShapeDtypeStruct(dims, dtype)


def kept(dtype, *dims):
    return pltpu.VMEM(dims, dtype)


def in_hbm(dtype, *dims):
    return pltpu.HBM(dims, dtype)


def from_hbm(value):
    return pltpu.with_memory_space_constraint(value, pltpu.HBM)


def where_am_i():
    head = lax.axis_index("head")
    return head & 1, (head >> 1) & 1, head >> 2, lax.axis_index("section")


def kernel_call(body, name, args, outs, scratch=(), scalars=0, loose=0, flops=0, limit=16):
    moved = sum(a.size * a.dtype.itemsize for a in args)
    return pl.pallas_call(
        body,
        in_specs=[SMEM] * scalars + [VMEM] * (len(args) - scalars - loose) + [ANYWHERE] * loose,
        out_specs=[ANYWHERE if getattr(o, "memory_space", None) is pltpu.HBM else VMEM for o in outs],
        out_shape=list(outs),
        scratch_shapes=list(scratch),
        compiler_params=pltpu.CompilerParams(vmem_limit_bytes=limit * MIB),
        cost_estimate=pl.CostEstimate(flops=flops, bytes_accessed=moved, transcendentals=0),
        name=name,
    )(*args)


def lanes(i):
    return slice(i * DK, (i + 1) * DK)


def at_rows(start, count):
    return pl.ds(pl.multiple_of(start, count), count)


def run_copies(pairs, sems):
    copies = [pltpu.make_async_copy(src, dst, sems.at[i]) for i, (src, dst) in enumerate(pairs)]
    for copy in copies:
        copy.start()
    for copy in copies:
        copy.wait()


def pick_held(slots, store, out, sems):
    mirror = lax.axis_size("section") - 1 - lax.axis_index("section")
    run_copies([(store.at[slots[t, mirror]], out.at[t]) for t in range(TICKS)], sems)


def pick_rows(current, upstream, tokens, cotangents, z, *refs):
    *fresh, sems = refs
    core, _, column, _ = where_am_i()
    rows = z.shape[0] // 2
    at = at_rows(core * (current.shape[0] // 2) + column * rows, rows)
    pairs = [(current.at[at, :], z.at[:rows, :]), (upstream.at[at, :], z.at[rows:, :])]
    for t in range(TICKS):
        pairs.append((tokens.at[t, at, :], fresh[t].at[:rows, :]))
        pairs.append((cotangents.at[t, at, :], fresh[t].at[rows:, :]))
    run_copies(pairs, sems)


def turn_first(slots, current, gain, shares, flag, current_out, gain_out, turned):
    section, head = lax.axis_index("section"), lax.axis_index("head")
    share = shares.shape[1]
    turned[...] = current[...].T
    shares[0] = turned[at_rows(head * share, share), :]
    shares[1] = turned[at_rows((head ^ 2) * share, share), :]
    same = jnp.where(slots[0, section] == slots[1, section], 1.0, 0.0)
    flag[...] = jnp.full(flag.shape, same, F32)
    current_out[...] = current[...]
    gain_out[...] = gain[...]


def pick_reload(near, far, shares, flag, both):
    both[0] = near[0]
    both[1] = far[0]
    same = flag[0:1, :] > 0.5
    for y, ref in enumerate((near, far)):
        both[2 + y] = jnp.where(same, shares[y].astype(F32), ref[1].astype(F32)).astype(BF16)


def part_reload(own, got2, got1, got3, after, first, second):
    for j, ref in enumerate((own, got1, got2, got3)):
        first[2 * j : 2 * j + 2] = ref[0:2]
        second[2 * j : 2 * j + 2] = ref[2:4]


def pick_share(first_shares, current, out, turned):
    share = first_shares.shape[1]
    turned[...] = current[...].T
    out[0] = first_shares[0]
    out[1] = turned[at_rows(lax.axis_index("head") * share, share), :]


def attend_and_project(n, total, keep_ref, send_ref, wq, wk, wv, wo, q, k, v, context, ready):
    ready(0)
    q[...] = dot(n, wq[...]).astype(BF16)
    ready(1)
    k[...] = dot(n, wk[...]).astype(BF16)
    ready(2)
    v[...] = dot(n, wv[...]).astype(BF16)
    for i in range(q.shape[1] // DK):
        at = lanes(i)
        low = softmax(q[:, at], k[:, at]).astype(BF16)
        context[:, at] = dot(low, v[:, at]).astype(BF16)
    ready(3)
    total[...] = dot(context[...], wo[...])
    core = where_am_i()[0]
    half = keep_ref.shape[0]
    keep_ref[...] = total[at_rows(core * half, half), :]
    send_ref[...] = total[at_rows((1 - core) * half, half), :].astype(BF16)


def forward_first(rows, gain, hq, hk, hv, ho, wq, wk, wv, wo, keep, send, q, k, v, context, total, sems):
    copies = [
        pltpu.make_async_copy(src, dst, sems.at[i])
        for i, (src, dst) in enumerate(((hq, wq), (hk, wk), (hv, wv), (ho, wo)))
    ]
    for copy in copies:
        copy.start()
    n = normalize(rows[...], gain[...])[0].astype(BF16)
    attend_and_project(
        n, total, keep, send, wq, wk, wv, wo, q, k, v, context, lambda i: copies[i].wait()
    )


def put_pieces(pieces, first, second):
    core, _, column, _ = where_am_i()
    rows = pieces[0].shape[0] // 2
    half = first.shape[0] // 2
    for i, ref in enumerate(pieces):
        c = core if i < 4 else 1 - core
        at = at_rows(c * half + (column ^ (i % 4)) * rows, rows)
        first[at, :] = ref[:rows, :]
        second[at, :] = ref[rows:, :]


def forward_next(gain, wq, wk, wv, wo, *refs):
    pieces, (rows, g, keep, send), (q, k, v, context, total) = refs[:8], refs[8:12], refs[12:]
    put_pieces(pieces, rows, g)
    n = normalize(rows[...], gain[...])[0].astype(BF16)
    attend_and_project(n, total, keep, send, wq, wk, wv, wo, q, k, v, context, lambda i: None)


def put_last(slots, store, arrived, gain_rows, gain_other, *refs):
    pieces, (rows, g, stored, gain_out) = refs[:8], refs[8:]
    mirror = lax.axis_size("section") - 1 - lax.axis_index("section")
    stored[...] = store[...]
    for t in range(TICKS):
        stored[slots[t, mirror]] = arrived[t]
    put_pieces(pieces, rows, g)
    value = get_gain(gain_rows, 0) + get_gain(gain_other, 0)
    share = gain_out.shape[1]
    for h in range(value.shape[1] // share):

        @pl.when(lax.axis_index("head") == h)
        def _():
            gain_out[...] = value[:, h * share : (h + 1) * share]


def recompute_kernel(gain, wq, wk, wv, *refs):
    mine, other, block_ref, normed_t, q, k, v, soft, context, block_t = refs
    core, high, column, _ = where_am_i()
    share = mine.shape[1]
    for ref, c in ((mine, core), (other, 1 - core)):
        for i in range(8):
            head = (column ^ (i // 2)) * 4 + (high ^ (i % 2)) * 2 + c
            block_t[at_rows(head * share, share), :] = ref[i]
    block = block_t[...].T
    block_ref[...] = block
    n = normalize(block, gain[...])[0].astype(BF16)
    normed_t[...] = n.T
    q[...] = dot(n, wq[...]).astype(BF16)
    k[...] = dot(n, wk[...]).astype(BF16)
    v[...] = dot(n, wv[...]).astype(BF16)
    for i in range(q.shape[1] // DK):
        at = lanes(i)
        rows = softmax(q[:, at], k[:, at])
        soft[i] = rows
        context[:, at] = dot(rows.astype(BF16), v[:, at]).astype(BF16)


def backward_kernel(
    g, block, gain, q, k, v, soft, wq, wk, wv, wo, ahead_keep, ahead_send, gain_before,
    *refs,
):
    keep, send, qg, kg, vg, gain_part, grads, total = refs
    grads[...] = dot_nt(g[...], wo[...]).astype(BF16)
    for i in range(q.shape[1] // DK):
        at = lanes(i)
        rows = soft[i]
        grad = grads[:, at]
        soft_grad = dot_nt(grad, v[:, at])
        vg[:, at] = dot_tn(rows.astype(BF16), grad).astype(BF16)
        along = jnp.sum(rows * soft_grad, axis=-1, keepdims=True)
        score_grad = (rows * (soft_grad - along) * SCALE).astype(BF16)
        qg[:, at] = dot(score_grad, k[:, at]).astype(BF16)
        kg[:, at] = dot_tn(score_grad, q[:, at]).astype(BF16)
    total[...] = dot_nt(qg[...], wq[...])
    total[...] += dot_nt(kg[...], wk[...])
    total[...] += dot_nt(vg[...], wv[...])
    half = ahead_keep.shape[0]
    core = where_am_i()[0]
    keep[:half, :] = ahead_keep[...]
    keep[half:, :] = total[at_rows(core * half, half), :]
    send[:half, :] = ahead_send[...]
    send[half : 2 * half, :] = total[at_rows((1 - core) * half, half), :].astype(BF16)
    unit = normalize(block[...], gain[...])[1]
    part = gain_before[...] + jnp.sum(total[...] * unit, axis=0, keepdims=True)
    gain_part[...] = part
    if send.shape[0] > 2 * half:
        put_gain(send, 2 * half, part)


def put_gain(ref, row, value):
    value = jnp.broadcast_to(value, (16, value.shape[1]))
    high = value.astype(BF16)
    low = (value - high.astype(F32)).astype(BF16)
    is_first = lax.broadcasted_iota(jnp.int32, value.shape, 0) == 0
    ref[row : row + 16, :] = jnp.where(is_first, high.astype(F32), low.astype(F32)).astype(BF16)


def get_gain(ref, row):
    tile = ref[row : row + 16, :].astype(F32)
    return tile[0:1] + tile[1:2]


def after_core(keep, got, gain_part, *refs):
    own, to1, to2, to3, gain_out, mine = refs[-6:]
    column = where_am_i()[2]
    half = keep.shape[0] // 2
    rows = half // 4
    mine[...] = keep[...] + got[: 2 * half, :].astype(F32)
    for j, ref in ((0, own), (1, to1), (2, to2), (3, to3)):
        for part in range(2):
            at = at_rows(part * half + (column ^ j) * rows, rows)
            ref[part * rows : (part + 1) * rows, :] = mine[at, :].astype(ref.dtype)
    if got.shape[0] > 2 * half:
        value = gain_part[...] + get_gain(got, 2 * half)
        gain_out[...] = value
        for ref in (to1, to2, to3):
            put_gain(ref, 2 * rows, value)
    else:
        gain_out[...] = gain_part[...]


def after_column(own, z, block, gain, gain_part, got2, got1, got3, *refs):
    even, odd, gain_out = refs[-3:]
    core, high, column, section = where_am_i()
    rows = z.shape[0] // 2
    tokens = block.shape[0]
    total = [None, None]
    for part in range(2):
        at = slice(part * rows, (part + 1) * rows)
        total[part] = own[at, :] + (
            got1[at, :].astype(F32) + (got2[at, :].astype(F32) + got3[at, :].astype(F32))
        )
    here = jnp.where(high == 0, 1.0, 0.0).astype(F32)
    ahead = (here * z[:rows, :].astype(F32) + total[0]).astype(BF16)
    at = at_rows(core * (tokens // 2) + column * rows, rows)
    _, unit, inverse = normalize(block[at, :], gain[...])
    unit_grad = total[1] * gain[...]
    along = jnp.mean(unit_grad * unit, axis=-1, keepdims=True)
    back = here * z[rows:, :].astype(F32) + inverse * (unit_grad - unit * along)
    back = back.astype(BF16)

    @pl.when((section & 1) == 0)
    def _():
        even[...] = ahead
        odd[...] = back

    @pl.when((section & 1) == 1)
    def _():
        even[...] = back
        odd[...] = ahead

    if got1.shape[0] > 2 * rows:
        value = get_gain(got1, 2 * rows) + get_gain(got2, 2 * rows) + get_gain(got3, 2 * rows)
        put_gain(gain_out, 0, gain_part[...] + value)
    else:
        put_gain(gain_out, 0, gain_part[...])


def after_shift(even1, even0, odd1, odd0, fresh, *refs):
    z = refs[-1]
    section = where_am_i()[3]
    rows = even0.shape[0]
    even = (even0[...].astype(F32) + even1[...].astype(F32)).astype(BF16)
    odd = (odd0[...].astype(F32) + odd1[...].astype(F32)).astype(BF16)

    @pl.when((section & 1) == 0)
    def _():
        z[:rows, :] = odd
        z[rows:, :] = even

    @pl.when((section & 1) == 1)
    def _():
        z[:rows, :] = even
        z[rows:, :] = odd

    @pl.when(section == 0)
    def _():
        z[:rows, :] = fresh[:rows, :]

    @pl.when(section == lax.axis_size("section") - 1)
    def _():
        z[rows:, :] = fresh[rows:, :]


def step_block(ref, axis):
    size = ref.shape[axis] // pl.num_programs(0)
    at = pl.ds(pl.multiple_of(pl.program_id(0) * size, size), size)
    return ref[at, :] if axis == 0 else ref[:, at]


def in_weight_kernel(after, n0, n1, *refs):
    left, right = step_block(n0, 0), step_block(n1, 0)
    for i in range(3):
        refs[6 + i][...] = (dot(left, refs[2 * i][...]) + dot(right, refs[2 * i + 1][...])).astype(BF16)


def out_weight_kernel(after, c0, c1, g0, g1, out):
    out[...] = (dot_tn(step_block(c0, 1), g0[...]) + dot_tn(step_block(c1, 1), g1[...])).astype(BF16)


def weight_grads(body, name, after, args, rows, count):
    steps = 4
    tokens, cols = args[-1].shape
    return pl.pallas_call(
        body,
        grid=(steps,),
        in_specs=[pl.BlockSpec(memory_space=pl.ANY)] + [VMEM] * len(args),
        out_specs=[pl.BlockSpec((rows // steps, cols), lambda i: (i, 0))] * count,
        out_shape=[shape(BF16, rows, cols)] * count,
        compiler_params=pltpu.CompilerParams(
            dimension_semantics=("arbitrary",), vmem_limit_bytes=16 * MIB
        ),
        cost_estimate=pl.CostEstimate(
            flops=4 * count * tokens * rows * cols, bytes_accessed=2 * count * rows * cols, transcendentals=0
        ),
        name=name,
    )(after, *args)


class Moves:
    def __init__(self, sections, heads):
        self.sections, self.heads = sections, heads

    def send(self, value, to, mask):
        pairs = []
        for s in range(self.sections):
            t = to(s)
            if 0 <= t < self.sections:
                pairs += [(s * self.heads + h, t * self.heads + (h ^ mask)) for h in range(self.heads)]
        return lax.ppermute(value, ("section", "head"), pairs)

    def flip(self, value, mask):
        return self.send(value, lambda s: s, mask)

    def even(self, value, mask):
        return self.send(value, lambda s: s ^ 1, mask)

    def odd(self, value, mask):
        return self.send(value, lambda s: ((s - 1) ^ 1) + 1, mask)

    def mirror(self, value, mask):
        return self.send(value, lambda s: self.sections - 1 - s, mask)


def per_device(
    section_inputs, section_cotangents, fresh_tokens, fresh_cotangents, norm_gain,
    query_weight, key_weight, value_weight, out_weight, saved_inputs, reload_slot,
):
    sections, heads = lax.axis_size("section"), lax.axis_size("head")
    section, head = lax.axis_index("section"), lax.axis_index("head")
    moves = Moves(sections, heads)
    share = saved_inputs.shape[3]
    gain = norm_gain
    store = jnp.swapaxes(saved_inputs[0], 1, 2)
    tokens, width = section_inputs.shape[1:]
    inner = query_weight.shape[2]
    half, rows = tokens // 2, tokens // 8
    unit_flops = 2 * tokens * width * inner
    current, upstream = section_inputs[0], section_cotangents[0]

    (going,) = kernel_call(
        pick_held, "pick_held", (reload_slot, from_hbm(store)), [kept(BF16, TICKS, share, tokens)],
        [pltpu.SemaphoreType.DMA((TICKS,))], 1, 1,
    )
    near, far = moves.mirror(going, 0), moves.mirror(going, 2)
    z, *fresh = kernel_call(
        pick_rows, "pick_rows",
        [from_hbm(a) for a in (current, upstream, fresh_tokens, fresh_cotangents)],
        [kept(BF16, 2 * rows, width)] * (1 + TICKS),
        [pltpu.SemaphoreType.DMA((2 + 2 * TICKS,))], 0, 4,
    )
    first_shares, flag, first_inputs, gain = kernel_call(
        turn_first, "turn_first", (reload_slot, current, gain),
        [
            kept(BF16, 2, share, tokens), kept(F32, 8, tokens),
            kept(BF16, tokens, width), kept(F32, 1, width),
        ],
        [pltpu.VMEM((width, tokens), BF16)], 1,
    )
    (both,) = kernel_call(
        pick_reload, "pick_reload", (near, far, first_shares, flag),
        [kept(BF16, 2 * TICKS, share, tokens)],
    )
    far_shares = moves.flip(both, 8)
    arriving = [both, far_shares, moves.flip(both, 4), moves.flip(both, 12)]

    flat = kept(BF16, tokens, inner)
    whole = kept(BF16, tokens, width)
    half_outs = [kept(F32, half, width), kept(BF16, half, width)]
    work = [pltpu.VMEM((tokens, inner), BF16)] * 4 + [pltpu.VMEM((tokens, width), F32)]
    gain_part = jnp.zeros((1, width), F32)
    left, context, grads_of, cotangents = [], [], [], []
    pieces = None

    def recompute(u):
        return kernel_call(
            recompute_kernel, "recompute", (gain, wq, wk, wv, *reload[u]),
            [
                whole, kept(BF16, width, tokens), flat, flat, flat,
                kept(F32, inner // DK, tokens, tokens), flat,
            ],
            [pltpu.VMEM((width, tokens), BF16)], 0, 0, 5 * unit_flops,
        )

    for t in range(TICKS):
        if t == 0:
            raw = [
                from_hbm(w[0]) for w in (query_weight, key_weight, value_weight, out_weight)
            ]
            *weights, keep, send = kernel_call(
                forward_first, "forward_first", (first_inputs, gain, *raw),
                [kept(BF16, *w.shape) for w in raw] + half_outs,
                work + [pltpu.SemaphoreType.DMA((4,))], 0, 4, 5 * unit_flops,
            )
            wq, wk, wv, wo = weights
            own_shares = kernel_call(
                part_reload, "part_reload", (*arriving, send),
                [kept(BF16, 8, share, tokens)] * TICKS, (), 0, 1,
            )
            reload = [(a, moves.flip(a, 1)) for a in own_shares]
        else:
            current, upstream, keep, send = kernel_call(
                forward_next, "forward_next", (gain, wq, wk, wv, wo, *pieces),
                [whole] * 2 + half_outs, work, 0, 0, 5 * unit_flops,
            )
        if t == 0:
            read = [recompute(u) for u in range(1)]
        block, normed_t, q, k, v, soft, ctx = read[t]
        extra = 16 if t == TICKS - 1 else 0
        keep, send, qg, kg, vg, gain_part = kernel_call(
            backward_kernel, "backward",
            (upstream, block, gain, q, k, v, soft, wq, wk, wv, wo, keep, send, gain_part),
            [kept(F32, tokens, width), kept(BF16, tokens + extra, width)]
            + [flat] * 3 + [kept(F32, 1, width)],
            [pltpu.VMEM((tokens, inner), BF16), pltpu.VMEM((tokens, width), F32)],
            0, 0, 6 * unit_flops,
        )
        left.append(normed_t)
        context.append(ctx)
        grads_of.append((qg, kg, vg))
        cotangents.append(upstream)

        got = moves.flip(send, 1)
        last = t == TICKS - 1
        if last:
            (shares,) = kernel_call(
                pick_share, "pick_share", (first_shares, current), [kept(BF16, 2, share, tokens)],
                [pltpu.VMEM((width, tokens), BF16)],
            )
            arrived = moves.mirror(shares, 0)
        beside = [shares] if last else []
        own, to1, to2, to3, gain_sum = kernel_call(
            after_core, "after_core", (keep, got, gain_part, *beside),
            [kept(F32, 2 * rows, width)] + [kept(BF16, 2 * rows + extra, width)] * 3 + [kept(F32, 1, width)],
            [pltpu.VMEM((tokens, width), F32)], 0, len(beside),
        )
        got2 = moves.flip(to2, 8)
        got1, got3 = moves.flip(to1, 4), moves.flip(to3, 12)
        if last:
            query_grad, key_grad, value_grad = weight_grads(
                in_weight_kernel, "in_grads", own,
                [*left, *[grads_of[u][i] for i in range(3) for u in range(TICKS)]], width, 3,
            )
            beside = [from_hbm(query_grad), arrived]
        else:
            read.append(recompute(1))
            beside = [read[1][5]]
        even, odd, gain_rows = kernel_call(
            after_column, "after_column",
            (own, z, block, gain, gain_sum, got2, got1, got3, *beside),
            [kept(BF16, rows, width)] * 2 + [kept(BF16, 16, width)], (), 0, len(beside),
        )
        even0, odd0 = moves.even(even, 0), moves.odd(odd, 0)
        even1, odd1 = moves.even(even, 2), moves.odd(odd, 2)
        if last:
            (out_grad,) = weight_grads(
                out_weight_kernel, "out_grad", even, [*context, *cotangents], inner, 1
            )
            gain_other = moves.flip(gain_rows, 2)
            beside = [gain_other, from_hbm(out_grad)]
        else:
            beside = []
        (z,) = kernel_call(
            after_shift, "after_shift", (even1, even0, odd1, odd0, fresh[t], *beside),
            [kept(BF16, 2 * rows, width)], (), 0, len(beside),
        )
        pieces = [z] + [moves.flip(z, 4 * j) for j in (1, 2, 3)]
        pieces = pieces + [moves.flip(p, 1) for p in pieces]
    last_inputs, last_cotangents, stored, gain_grad = kernel_call(
        put_last, "put_last", (reload_slot, store, arrived, gain_rows, gain_other, *pieces),
        [shape(BF16, tokens, width)] * 2 + [shape(BF16, *store.shape), shape(F32, 1, share)], (), 1,
    )
    return (
        last_inputs[None],
        last_cotangents[None],
        jnp.swapaxes(stored, 1, 2)[None],
        query_grad[None],
        key_grad[None],
        value_grad[None],
        out_grad[None],
        gain_grad,
    )


def solution(mesh):
    placed = (
        P("section", None, None),
        P("section", None, None),
        P(),
        P(),
        P("section", None),
        P("section", None, "head"),
        P("section", None, "head"),
        P("section", None, "head"),
        P("section", "head", None),
        P("section", None, None, "head"),
        P(),
    )
    return jax.shard_map(
        per_device,
        mesh=mesh,
        in_specs=placed,
        out_specs=(
            P("section", None, None),
            P("section", None, None),
            P("section", None, None, "head"),
            P("section", None, "head"),
            P("section", None, "head"),
            P("section", None, "head"),
            P("section", "head", None),
            P("section", "head"),
        ),
        check_vma=False,
    )
```
